32 devices in a mesh: replica: 8 (over z, core), tensor: 4 (over y, x).
Axes of the slice: x: 2, y: 2, z: 4, core: 2. Of those that a mesh axis runs over, the one named last changes fastest.
Arguments:
- features: bfloat16 [10240, 5120], P('replica', 'tensor'), may hold values from -6 to 6
- key_grad: bfloat16 [10240, 512], P(('replica', 'tensor')), may hold values from -0.29882812 to 0.29882812
- master: float32 [8, 5120, 512], P('replica', 'tensor'), may hold values from -6 to 6
- exponents: int32 [2], replicated, may hold values from 0 to 2, as said below
Outputs:
- new_master: float32 [8, 5120, 512], P('replica', 'tensor')
- new_working: bfloat16 [8, 5120, 512], P('replica', 'tensor')
- input_grad: bfloat16 [10240, 5120], P('replica', 'tensor')
The draws below stay inside these ranges and needn't reach their ends.
Inputs may be any that keep to these rules, and one draw needn't show every extreme that they name: Two different exponents: one of them is always 5 (the top bit of 8), the other lies in 0 to 4; either may come first.
All inputs are finite; a program needn't handle non-finite values.
Results may differ from the reference program's by a relative error of at most 0.006.
Values may be sent and summed in bfloat16 or wider, within the bound.
A program may use at most 64 MiB of HBM per device.

```python
import jax
import jax.numpy as jnp
from jax import lax

D = 5120
KVW = 512
TOKENS = 10240
N_REPLICA = 8


def draw_exponents(key, part):
    bit_count = N_REPLICA.bit_length() - 1
    top_bit = jnp.int32(bit_count - 1)
    other_bit = jax.random.randint(jax.random.fold_in(key, 11), (), 0, bit_count - 1).astype(jnp.int32)
    order_flag = jax.random.randint(jax.random.fold_in(key, 12), (), 0, 2).astype(jnp.int32)
    first_bit = jnp.where(order_flag == 0, top_bit, other_bit)
    second_bit = jnp.where(order_flag == 0, other_bit, top_bit)
    return jnp.stack([first_bit, second_bit]).astype(jnp.int32)


def block_scale(stream_key, extent, pieces, smallest, largest):
    gain, own = 1.0, jax.random.fold_in(stream_key, 6)
    for dim, blocks in pieces:
        draws = jnp.exp(jax.random.uniform(jax.random.fold_in(own, dim), (blocks,), jnp.float32, smallest / len(pieces), largest / len(pieces)))
        gain = gain * jnp.repeat(draws, extent[dim] // blocks).reshape([-1 if axis == dim else 1 for axis in range(len(extent))])
    return gain


def gaussian(key, dims, scale, limit, cuts=(), kind=jnp.bfloat16):
    drawn = scale * jax.random.normal(key, dims, jnp.float32)
    if cuts:
        drawn = drawn * block_scale(key, dims, cuts, -0.22, 0.18)
    return jnp.clip(drawn, -limit, limit).astype(kind)


def setup_inputs(seed: int = 0) -> dict:
    streams_of = jax.random.split(jax.random.key(seed), 5)
    return {
        "features": gaussian(streams_of[0], (TOKENS, D), 1.0, 6.0, ((0, 8), (1, 4))),
        "key_grad": gaussian(streams_of[1], (TOKENS, KVW), 0.0442, 0.29882812, ((0, 32),)),
        "master": gaussian(streams_of[2], (N_REPLICA, D, KVW), 1.0, 6.0, ((0, 8), (1, 4)), jnp.float32),
        "exponents": draw_exponents(jax.random.fold_in(streams_of[4], 71), 0),
    }


step_rate = 0.2


def replica_step(triple):
    features_r, key_grad_r, master_r = triple
    weight_grad = jnp.dot(features_r.T, key_grad_r, preferred_element_type=jnp.float32)
    working = master_r.astype(jnp.bfloat16)
    input_rows = jnp.dot(key_grad_r, working.T, preferred_element_type=jnp.float32).astype(jnp.bfloat16)
    stepped = master_r - step_rate * weight_grad
    return stepped, input_rows


def reference(features, key_grad, master, exponents):
    groups = master.shape[0]
    grouped_feat = features.reshape(groups, -1, features.shape[1])
    grouped_grad = key_grad.reshape(groups, -1, key_grad.shape[1])
    stepped, input_rows = lax.map(replica_step, (grouped_feat, grouped_grad, master))
    indices = jnp.arange(groups, dtype=jnp.int32)
    for which_round in range(2):
        partner = jnp.bitwise_xor(indices, jnp.left_shift(jnp.int32(1), exponents[which_round].astype(jnp.int32)))
        stepped = 0.5 * (stepped + jnp.take(stepped, partner, axis=0))
    return stepped, stepped.astype(jnp.bfloat16), input_rows.reshape(-1, features.shape[1])
```

```python
from functools import partial

import jax
import jax.numpy as jnp
from jax import lax
from jax.experimental import pallas as pl
from jax.experimental.pallas import tpu as pltpu
from jax.sharding import PartitionSpec as P

MESH = pl.DeviceIdType.MESH
step_rate = 0.2
LANES = 128
TURN = 256


def remote(src, dst, send_sem, recv_sem, device):
    return pltpu.make_async_remote_copy(
        src_ref=src, dst_ref=dst, send_sem=send_sem, recv_sem=recv_sem,
        device_id=device, device_id_type=MESH,
    )


def kernel(
    bit, top, n_tensor, parts, lag,
    feat_hbm, grad_hbm, master_hbm,
    mean_hbm, input_hbm,
    feat, feat_t, grads, master, working, outgoing, first_in, second_in, partial_sum, mean, rows_out,
    load_sem, grad_send, grad_recv, out_sem, rows_sem,
    send_a, recv_a, send_b, recv_b, send_c, recv_c,
):
    replica, tensor = lax.axis_index("replica"), lax.axis_index("tensor")
    tokens, width = feat.shape
    columns = grads.shape[1]
    shard_tokens = grad_hbm.shape[0]
    n_cols = columns // LANES
    chain = bit == top - 1
    low = replica // (1 << bit) % 2
    high = replica // (1 << top) % 2
    near = {"replica": replica + (1 - 2 * low) * (1 << bit), "tensor": tensor}
    far_step = (1 - 2 * high) * (1 << top)
    if chain:
        inner = low != high
        far = {"replica": replica + (1 - 2 * high) * (1 << bit), "tensor": tensor}
    else:
        far = {"replica": replica + far_step, "tensor": tensor}

    def peer(d):
        return lax.rem(tensor + d, n_tensor)

    feat_loads = []
    for b in range(tokens // TURN):
        block = pl.ds(b * TURN, TURN)
        feat_loads.append(pltpu.make_async_copy(feat_hbm.at[block], feat.at[block], load_sem.at[b]))
    master_load = pltpu.make_async_copy(master_hbm, master, load_sem.at[tokens // TURN])
    own_rows = pl.ds(pl.multiple_of(tensor * shard_tokens, 16), shard_tokens)
    own_grads = pltpu.make_async_copy(grad_hbm, grads.at[own_rows], load_sem.at[tokens // TURN + 1])
    for load in feat_loads:
        load.start()
    own_grads.start()
    master_load.start()

    barrier = pltpu.get_barrier_semaphore()
    for d in range(1, n_tensor):
        pl.semaphore_signal(barrier, inc=1, device_id={"replica": replica, "tensor": peer(d)}, device_id_type=MESH)
    pl.semaphore_signal(barrier, inc=1, device_id=near, device_id_type=MESH)
    if chain:
        @pl.when(inner)
        def _():
            pl.semaphore_signal(barrier, inc=1, device_id=far, device_id_type=MESH)
            pl.semaphore_wait(barrier, n_tensor + 1)

        @pl.when(jnp.logical_not(inner))
        def _():
            pl.semaphore_wait(barrier, n_tensor)
    else:
        pl.semaphore_signal(barrier, inc=1, device_id=far, device_id_type=MESH)
        pl.semaphore_wait(barrier, n_tensor + 1)

    def grad_copy(j, d, sending):
        source = tensor if sending else lax.rem(tensor + n_tensor - d, n_tensor)
        cols = pl.ds(pl.multiple_of(j * LANES, LANES), LANES)
        rows = pl.ds(pl.multiple_of(source * shard_tokens, 16), shard_tokens)
        return remote(
            grad_hbm.at[:, cols], grads.at[rows, cols], grad_send.at[j, d - 1], grad_recv.at[j, d - 1],
            {"replica": replica, "tensor": peer(d)},
        )

    def send_grads(j, carry):
        for d in range(1, n_tensor):
            grad_copy(j, d, True).start()
        return carry

    lax.fori_loop(0, n_cols, send_grads, 0)

    for b in range(tokens // TURN):
        feat_loads[b].wait()
        feat_t[:, b * TURN:(b + 1) * TURN] = feat[b * TURN:(b + 1) * TURN, :].T
    master_load.wait()
    working[...] = master[...].astype(jnp.bfloat16)
    own_grads.wait()

    span = width if chain else width // 2
    rows = span // parts
    steps = n_cols * parts

    def place(q, half=None):
        j = q // parts
        i = q - j * parts
        start = i * rows if half is None else half * span + i * rows
        return pl.ds(pl.multiple_of(start, 16), rows), pl.ds(pl.multiple_of(j * LANES, LANES), LANES)

    def wait_grads(q):
        @pl.when(lax.rem(q, parts) == 0)
        def _():
            for d in range(1, n_tensor):
                grad_copy(q // parts, d, False).wait_recv()

    def stepped(at):
        r, c = at
        weight_grad = jnp.dot(feat_t[r, :], grads[:, c], preferred_element_type=jnp.float32)
        return master[r, c] - step_rate * weight_grad

    def emit(q, at, value):
        r, c = at
        mean[r, c] = (0.25 * value).astype(jnp.bfloat16)
        pltpu.make_async_copy(mean.at[r, c], mean_hbm.at[r, c], out_sem.at[q]).start()
        remote(mean.at[r, c], mean_hbm.at[r, c], send_c.at[q], recv_c.at[q], near).start()

    n_blocks = 8
    block_tokens = tokens // n_blocks

    def input_copy(b):
        r = pl.ds(pl.multiple_of(b * block_tokens, 16), block_tokens)
        return pltpu.make_async_copy(rows_out.at[r], input_hbm.at[r], rows_sem.at[b])

    def input_block(b):
        r = pl.ds(pl.multiple_of(b * block_tokens, 16), block_tokens)
        rows_out[r, :] = lax.dot_general(
            grads[r, :], working[...], (((1,), (1,)), ((), ())), preferred_element_type=jnp.float32
        ).astype(jnp.bfloat16)
        input_copy(b).start()

    def loop(begin, end, body):
        def run(q, carry):
            body(q)
            return carry

        lax.fori_loop(begin, end, run, 0)

    if chain:
        def to_near(q):
            r, c = place(q)
            return remote(outgoing.at[r, c], first_in.at[r, c], send_a.at[q], recv_a.at[q], near)

        def to_far(q):
            r, c = place(q)
            return remote(outgoing.at[r, c], second_in.at[r, c], send_b.at[q], recv_b.at[q], far)

        def back(q):
            r, c = place(q)
            return remote(mean.at[r, c], mean_hbm.at[r, c], send_c.at[q], recv_c.at[q], near)

        @pl.when(jnp.logical_not(inner))
        def _():
            def give(q):
                wait_grads(q)
                r, c = place(q)
                outgoing[r, c] = stepped((r, c)).astype(jnp.bfloat16)
                to_near(q).start()

            loop(0, steps, give)
            loop(0, n_blocks, input_block)

            def settle(q):
                to_near(q).wait_send()
                back(q).wait_recv()

            loop(0, steps, settle)

        @pl.when(inner)
        def _():
            def finish(q):
                r, c = place(q)
                to_far(q).wait_recv()
                emit(q, (r, c), partial_sum[r, c] + second_in[r, c].astype(jnp.float32))

            def merge(q):
                wait_grads(q)
                r, c = place(q)
                own = stepped((r, c))
                to_near(q).wait_recv()
                own = own + first_in[r, c].astype(jnp.float32)
                partial_sum[r, c] = own
                outgoing[r, c] = own.astype(jnp.bfloat16)
                to_far(q).start()

                @pl.when(q >= lag)
                def _():
                    finish(q - lag)

                @pl.when(q >= steps - parts)
                def _():
                    for k in range(n_blocks // parts):
                        input_block((q - (steps - parts)) * (n_blocks // parts) + k)

            loop(0, steps, merge)
            loop(steps - lag, steps, finish)

            def settle(q):
                r, c = place(q)
                to_far(q).wait_send()
                back(q).wait_send()
                pltpu.make_async_copy(mean.at[r, c], mean_hbm.at[r, c], out_sem.at[q]).wait()

            loop(0, steps, settle)
    else:
        def to_near(q, half):
            r, c = place(q, half)
            return remote(outgoing.at[r, c], first_in.at[r, c], send_a.at[q], recv_a.at[q], near)

        def to_far(q):
            r, c = place(q, low)
            return remote(outgoing.at[r, c], second_in.at[r, c], send_b.at[q], recv_b.at[q], far)

        def back(q, half):
            r, c = place(q, half)
            return remote(mean.at[r, c], mean_hbm.at[r, c], send_c.at[q], recv_c.at[q], near)

        def merge(q):
            r, c = place(q, low)
            to_near(q, low).wait_recv()
            both = partial_sum[r, c] + first_in[r, c].astype(jnp.float32)
            partial_sum[r, c] = both
            outgoing[r, c] = both.astype(jnp.bfloat16)
            to_far(q).start()

        def give(q):
            wait_grads(q)
            r, c = place(q, 1 - low)
            outgoing[r, c] = stepped((r, c)).astype(jnp.bfloat16)
            to_near(q, 1 - low).start()
            r, c = place(q, low)
            partial_sum[r, c] = stepped((r, c))

            @pl.when(q >= 1)
            def _():
                merge(q - 1)

        loop(0, steps, give)
        merge(steps - 1)
        loop(0, n_blocks, input_block)

        def finish(q):
            r, c = place(q, low)
            to_far(q).wait_recv()
            emit(q, (r, c), partial_sum[r, c] + second_in[r, c].astype(jnp.float32))

        loop(0, steps, finish)

        def settle(q):
            r, c = place(q, low)
            to_near(q, 1 - low).wait_send()
            to_far(q).wait_send()
            back(q, low).wait_send()
            back(q, 1 - low).wait_recv()
            pltpu.make_async_copy(mean.at[r, c], mean_hbm.at[r, c], out_sem.at[q]).wait()

        loop(0, steps, settle)

    def settle_grads(j, carry):
        for d in range(1, n_tensor):
            grad_copy(j, d, True).wait_send()
        return carry

    lax.fori_loop(0, n_cols, settle_grads, 0)
    loop(0, n_blocks, lambda b: input_copy(b).wait())


def gossip(features, key_grad, shard, bit, top, n_tensor):
    tokens, width = features.shape
    columns = key_grad.shape[1]
    chain = bit == top - 1
    parts, lag = (4, 3) if chain else (2, 0)
    n_cols = columns // LANES
    steps = n_cols * parts
    dma = pltpu.SemaphoreType.DMA
    half, full = jnp.bfloat16, jnp.float32
    return pl.pallas_call(
        partial(kernel, bit, top, n_tensor, parts, lag),
        out_shape=(
            jax.ShapeDtypeStruct((width, columns), half),
            jax.ShapeDtypeStruct((tokens, width), half),
        ),
        in_specs=[pl.BlockSpec(memory_space=pl.ANY)] * 3,
        out_specs=[pl.BlockSpec(memory_space=pl.ANY)] * 2,
        scratch_shapes=[
            pltpu.VMEM((tokens, width), half),
            pltpu.VMEM((width, tokens), half),
            pltpu.VMEM((tokens, columns), half),
            pltpu.VMEM((width, columns), full),
            pltpu.VMEM((width, columns), half),
            pltpu.VMEM((width, columns), half),
            pltpu.VMEM((width, columns), half),
            pltpu.VMEM((width, columns), half),
            pltpu.VMEM((width, columns), full),
            pltpu.VMEM((width, columns), half),
            pltpu.VMEM((tokens, width), half),
            dma((tokens // TURN + 2,)),
            dma((n_cols, n_tensor - 1)),
            dma((n_cols, n_tensor - 1)),
            dma((steps,)),
            dma((8,)),
            dma((steps,)), dma((steps,)), dma((steps,)), dma((steps,)), dma((steps,)), dma((steps,)),
        ],
        compiler_params=pltpu.CompilerParams(
            collective_id=bit, has_side_effects=True, vmem_limit_bytes=48 * 1024 * 1024
        ),
        name=f"gossip_{bit}",
    )(features, key_grad, shard)


def solution(mesh):
    n_tensor = mesh.shape["tensor"]
    top = mesh.shape["replica"].bit_length() - 2

    def local(features, key_grad, master, exponents):
        which = jnp.minimum(exponents[0], exponents[1])
        branches = [partial(gossip, bit=bit, top=top, n_tensor=n_tensor) for bit in range(top)]
        mean, input_rows = lax.switch(which, branches, features, key_grad, master[0])
        return mean.astype(jnp.float32)[None], mean[None], input_rows

    in_specs = (
        P("replica", "tensor"),
        P(("replica", "tensor"), None),
        P("replica", "tensor", None),
        P(),
    )
    out_specs = (P("replica", "tensor", None), P("replica", "tensor", None), P("replica", "tensor"))
    return jax.shard_map(local, mesh=mesh, in_specs=in_specs, out_specs=out_specs, check_vma=False)
```

```python
from functools import partial

import jax
import jax.numpy as jnp
from jax import lax
from jax.experimental import pallas as pl
from jax.experimental.pallas import tpu as pltpu
from jax.sharding import PartitionSpec as P

MESH = pl.DeviceIdType.MESH
step_rate = 0.2
LANES = 128
TURN = 256


def remote(src, dst, send_sem, recv_sem, device):
    return pltpu.make_async_remote_copy(
        src_ref=src, dst_ref=dst, send_sem=send_sem, recv_sem=recv_sem,
        device_id=device, device_id_type=MESH,
    )


def kernel(
    bit, top, n_tensor, parts, lag,
    feat_hbm, grad_hbm, master_hbm,
    total_hbm, input_hbm,
    feat, feat_t, grads, master, working, outgoing, first_in, second_in, partial_sum, total, rows_out,
    load_sem, grad_send, grad_recv, out_sem, rows_sem,
    send_a, recv_a, send_b, recv_b, send_c, recv_c,
):
    replica, tensor = lax.axis_index("replica"), lax.axis_index("tensor")
    tokens, width = feat.shape
    columns = grads.shape[1]
    shard_tokens = grad_hbm.shape[0]
    n_cols = columns // LANES
    chain = bit == top - 1
    low = replica // (1 << bit) % 2
    high = replica // (1 << top) % 2
    near = {"replica": replica + (1 - 2 * low) * (1 << bit), "tensor": tensor}
    far_step = (1 - 2 * high) * (1 << top)
    if chain:
        inner = low != high
        far = {"replica": replica + (1 - 2 * high) * (1 << bit), "tensor": tensor}
    else:
        far = {"replica": replica + far_step, "tensor": tensor}

    def peer(d):
        return lax.rem(tensor + d, n_tensor)

    feat_loads = []
    for b in range(tokens // TURN):
        block = pl.ds(b * TURN, TURN)
        feat_loads.append(pltpu.make_async_copy(feat_hbm.at[block], feat.at[block], load_sem.at[b]))
    master_load = pltpu.make_async_copy(master_hbm, master, load_sem.at[tokens // TURN])
    own_rows = pl.ds(pl.multiple_of(tensor * shard_tokens, 16), shard_tokens)
    own_grads = pltpu.make_async_copy(grad_hbm, grads.at[own_rows], load_sem.at[tokens // TURN + 1])
    for load in feat_loads:
        load.start()
    own_grads.start()
    master_load.start()

    barrier = pltpu.get_barrier_semaphore()
    for d in range(1, n_tensor):
        pl.semaphore_signal(barrier, inc=1, device_id={"replica": replica, "tensor": peer(d)}, device_id_type=MESH)
    pl.semaphore_signal(barrier, inc=1, device_id=near, device_id_type=MESH)
    if chain:
        @pl.when(inner)
        def _():
            pl.semaphore_signal(barrier, inc=1, device_id=far, device_id_type=MESH)
            pl.semaphore_wait(barrier, n_tensor + 1)

        @pl.when(jnp.logical_not(inner))
        def _():
            pl.semaphore_wait(barrier, n_tensor)
    else:
        pl.semaphore_signal(barrier, inc=1, device_id=far, device_id_type=MESH)
        pl.semaphore_wait(barrier, n_tensor + 1)

    def grad_copy(j, d, sending):
        source = tensor if sending else lax.rem(tensor + n_tensor - d, n_tensor)
        cols = pl.ds(pl.multiple_of(j * LANES, LANES), LANES)
        rows = pl.ds(pl.multiple_of(source * shard_tokens, 16), shard_tokens)
        return remote(
            grad_hbm.at[:, cols], grads.at[rows, cols], grad_send.at[j, d - 1], grad_recv.at[j, d - 1],
            {"replica": replica, "tensor": peer(d)},
        )

    def send_grads(j, carry):
        for d in range(1, n_tensor):
            grad_copy(j, d, True).start()
        return carry

    send_grads(0, 0)

    for b in range(tokens // TURN):
        feat_loads[b].wait()
        feat_t[:, b * TURN:(b + 1) * TURN] = feat[b * TURN:(b + 1) * TURN, :].T
    master_load.wait()
    working[...] = master[...].astype(jnp.bfloat16)
    own_grads.wait()
    if n_cols > 1:
        send_grads(1, 0)

    span = width if chain else width // 2
    rows = span // parts
    steps = n_cols * parts

    def place(q, half=None):
        j = q // parts
        i = q - j * parts
        start = i * rows if half is None else half * span + i * rows
        return pl.ds(pl.multiple_of(start, 16), rows), pl.ds(pl.multiple_of(j * LANES, LANES), LANES)

    def wait_grads(q):
        @pl.when(lax.rem(q, parts) == 0)
        def _():
            for d in range(1, n_tensor):
                grad_copy(q // parts, d, False).wait_recv()

            @pl.when(q // parts + 2 < n_cols)
            def _():
                send_grads(q // parts + 2, 0)

    def stepped(at):
        r, c = at
        weight_grad = jnp.dot(feat_t[r, :], grads[:, c], preferred_element_type=jnp.float32)
        return master[r, c] - step_rate * weight_grad

    def emit(q, at, value):
        r, c = at
        total[r, c] = value.astype(jnp.bfloat16)
        pltpu.make_async_copy(total.at[r, c], total_hbm.at[r, c], out_sem.at[q]).start()
        remote(total.at[r, c], total_hbm.at[r, c], send_c.at[q], recv_c.at[q], near).start()

    n_blocks = 8
    block_tokens = tokens // n_blocks

    def input_copy(b):
        r = pl.ds(pl.multiple_of(b * block_tokens, 16), block_tokens)
        return pltpu.make_async_copy(rows_out.at[r], input_hbm.at[r], rows_sem.at[b])

    def input_block(b):
        r = pl.ds(pl.multiple_of(b * block_tokens, 16), block_tokens)
        rows_out[r, :] = lax.dot_general(
            grads[r, :], working[...], (((1,), (1,)), ((), ())), preferred_element_type=jnp.float32
        ).astype(jnp.bfloat16)
        input_copy(b).start()

    def input_blocks(q):
        @pl.when(q >= steps - parts)
        def _():
            for k in range(n_blocks // parts):
                input_block((q - (steps - parts)) * (n_blocks // parts) + k)

    def loop(begin, end, body):
        def run(q, carry):
            body(q)
            return carry

        lax.fori_loop(begin, end, run, 0)

    if chain:
        def to_near(q):
            r, c = place(q)
            return remote(outgoing.at[r, c], first_in.at[r, c], send_a.at[q], recv_a.at[q], near)

        def to_far(q):
            r, c = place(q)
            return remote(outgoing.at[r, c], second_in.at[r, c], send_b.at[q], recv_b.at[q], far)

        def back(q):
            r, c = place(q)
            return remote(total.at[r, c], total_hbm.at[r, c], send_c.at[q], recv_c.at[q], near)

        @pl.when(jnp.logical_not(inner))
        def _():
            def give(q):
                wait_grads(q)
                r, c = place(q)
                outgoing[r, c] = stepped((r, c)).astype(jnp.bfloat16)

                @pl.when(q >= 2)
                def _():
                    to_near(q - 2).wait_send()

                to_near(q).start()
                input_blocks(q)

            loop(0, steps, give)
            loop(steps - 2, steps, lambda q: to_near(q).wait_send())
            loop(0, steps, lambda q: back(q).wait_recv())

        @pl.when(inner)
        def _():
            def finish(q):
                r, c = place(q)
                to_far(q).wait_recv()
                emit(q, (r, c), partial_sum[r, c] + second_in[r, c].astype(jnp.float32))

            def merge(q):
                wait_grads(q)
                r, c = place(q)
                own = stepped((r, c))
                to_near(q).wait_recv()
                own = own + first_in[r, c].astype(jnp.float32)
                partial_sum[r, c] = own
                outgoing[r, c] = own.astype(jnp.bfloat16)
                to_far(q).start()

                @pl.when(q >= lag)
                def _():
                    finish(q - lag)

                input_blocks(q)

            loop(0, steps, merge)
            loop(steps - lag, steps, finish)

            def settle(q):
                r, c = place(q)
                to_far(q).wait_send()
                back(q).wait_send()
                pltpu.make_async_copy(total.at[r, c], total_hbm.at[r, c], out_sem.at[q]).wait()

            loop(0, steps, settle)
    else:
        def to_near(q, half):
            r, c = place(q, half)
            return remote(outgoing.at[r, c], first_in.at[r, c], send_a.at[q], recv_a.at[q], near)

        def to_far(q):
            r, c = place(q, low)
            return remote(outgoing.at[r, c], second_in.at[r, c], send_b.at[q], recv_b.at[q], far)

        def back(q, half):
            r, c = place(q, half)
            return remote(total.at[r, c], total_hbm.at[r, c], send_c.at[q], recv_c.at[q], near)

        def merge(q):
            r, c = place(q, low)
            to_near(q, low).wait_recv()
            both = partial_sum[r, c] + first_in[r, c].astype(jnp.float32)
            partial_sum[r, c] = both
            outgoing[r, c] = both.astype(jnp.bfloat16)

            @pl.when(q >= 2)
            def _():
                to_far(q - 2).wait_send()

            to_far(q).start()

        def finish(q):
            r, c = place(q, low)
            to_far(q).wait_recv()
            emit(q, (r, c), partial_sum[r, c] + second_in[r, c].astype(jnp.float32))

        def give(q):
            wait_grads(q)
            r, c = place(q, 1 - low)
            outgoing[r, c] = stepped((r, c)).astype(jnp.bfloat16)
            to_near(q, 1 - low).start()
            r, c = place(q, low)
            partial_sum[r, c] = stepped((r, c))

            @pl.when(q >= 1)
            def _():
                merge(q - 1)

            input_blocks(q)

            @pl.when(q >= lag)
            def _():
                finish(q - lag)

        loop(0, steps, give)
        merge(steps - 1)
        loop(steps - lag, steps, finish)
        loop(steps - 2, steps, lambda q: to_far(q).wait_send())

        def settle(q):
            r, c = place(q, low)
            to_near(q, 1 - low).wait_send()
            back(q, low).wait_send()
            back(q, 1 - low).wait_recv()
            pltpu.make_async_copy(total.at[r, c], total_hbm.at[r, c], out_sem.at[q]).wait()

        loop(0, steps, settle)

    def settle_grads(j, carry):
        for d in range(1, n_tensor):
            grad_copy(j, d, True).wait_send()
        return carry

    lax.fori_loop(0, n_cols, settle_grads, 0)
    loop(0, n_blocks, lambda b: input_copy(b).wait())


def gossip(features, key_grad, shard, bit, top, n_tensor):
    tokens, width = features.shape
    columns = key_grad.shape[1]
    chain = bit == top - 1
    parts, lag = (4, 3) if chain else (2, 3)
    n_cols = columns // LANES
    steps = n_cols * parts
    dma = pltpu.SemaphoreType.DMA
    half, full = jnp.bfloat16, jnp.float32
    return pl.pallas_call(
        partial(kernel, bit, top, n_tensor, parts, lag),
        out_shape=(
            jax.ShapeDtypeStruct((width, columns), half),
            jax.ShapeDtypeStruct((tokens, width), half),
        ),
        in_specs=[pl.BlockSpec(memory_space=pl.ANY)] * 3,
        out_specs=[pl.BlockSpec(memory_space=pl.ANY)] * 2,
        scratch_shapes=[
            pltpu.VMEM((tokens, width), half),
            pltpu.VMEM((width, tokens), half),
            pltpu.VMEM((tokens, columns), half),
            pltpu.VMEM((width, columns), full),
            pltpu.VMEM((width, columns), half),
            pltpu.VMEM((width, columns), half),
            pltpu.VMEM((width, columns), half),
            pltpu.VMEM((width, columns), half),
            pltpu.VMEM((width, columns), full),
            pltpu.VMEM((width, columns), half),
            pltpu.VMEM((tokens, width), half),
            dma((tokens // TURN + 2,)),
            dma((n_cols, n_tensor - 1)),
            dma((n_cols, n_tensor - 1)),
            dma((steps,)),
            dma((8,)),
            dma((steps,)), dma((steps,)), dma((steps,)), dma((steps,)), dma((steps,)), dma((steps,)),
        ],
        compiler_params=pltpu.CompilerParams(
            collective_id=bit, has_side_effects=True, vmem_limit_bytes=48 * 1024 * 1024
        ),
        name=f"gossip_{bit}",
    )(features, key_grad, shard)


def write_outputs(total, input_in, master_out, working_out, input_out):
    mean = 0.25 * total[...].astype(jnp.float32)
    master_out[...] = mean
    working_out[...] = mean.astype(jnp.bfloat16)
    input_out[...] = input_in[...]


def outputs(total, input_rows, pieces=5):
    width, columns = total.shape
    tokens = input_rows.shape[0]
    weights = pl.BlockSpec((width // pieces, columns), lambda i: (i, 0))
    inputs = pl.BlockSpec((tokens // pieces, width), lambda i: (i, 0))
    return pl.pallas_call(
        write_outputs,
        grid=(pieces,),
        out_shape=(
            jax.ShapeDtypeStruct((width, columns), jnp.float32),
            jax.ShapeDtypeStruct((width, columns), jnp.bfloat16),
            jax.ShapeDtypeStruct((tokens, width), jnp.bfloat16),
        ),
        in_specs=[weights, inputs],
        out_specs=[weights, weights, inputs],
        compiler_params=pltpu.CompilerParams(vmem_limit_bytes=32 * 1024 * 1024),
        name="write_outputs",
    )(total, input_rows)


def solution(mesh):
    n_tensor = mesh.shape["tensor"]
    top = mesh.shape["replica"].bit_length() - 2

    def local(features, key_grad, master, exponents):
        which = jnp.minimum(exponents[0], exponents[1])
        branches = [partial(gossip, bit=bit, top=top, n_tensor=n_tensor) for bit in range(top)]
        total, input_rows = lax.switch(which, branches, features, key_grad, master[0])
        new_master, new_working, input_grad = outputs(total, input_rows)
        return new_master[None], new_working[None], input_grad

    in_specs = (
        P("replica", "tensor"),
        P(("replica", "tensor"), None),
        P("replica", "tensor", None),
        P(),
    )
    out_specs = (P("replica", "tensor", None), P("replica", "tensor", None), P("replica", "tensor"))
    return jax.shard_map(local, mesh=mesh, in_specs=in_specs, out_specs=out_specs, check_vma=False)
```

```python
from functools import partial

import jax
import jax.numpy as jnp
from jax import lax
from jax.experimental import pallas as pl
from jax.experimental.pallas import tpu as pltpu
from jax.sharding import PartitionSpec as P

MESH = pl.DeviceIdType.MESH
step_rate = 0.2
LANES = 128
TURN = 256


def remote(src, dst, send_sem, recv_sem, device):
    return pltpu.make_async_remote_copy(
        src_ref=src, dst_ref=dst, send_sem=send_sem, recv_sem=recv_sem,
        device_id=device, device_id_type=MESH,
    )


def kernel(
    bit, top, n_tensor, parts, lag,
    feat_hbm, grad_hbm, master_hbm,
    total_hbm, input_hbm,
    feat, feat_t, grads, master, working, outgoing, first_in, second_in, partial_sum, total, rows_out,
    load_sem, grad_send, grad_recv, out_sem, rows_sem,
    send_a, recv_a, send_b, recv_b, send_c, recv_c,
):
    replica, tensor = lax.axis_index("replica"), lax.axis_index("tensor")
    tokens, width = feat.shape
    columns = grads.shape[1]
    shard_tokens = grad_hbm.shape[0]
    n_cols = columns // LANES
    chain = bit == top - 1
    low = replica // (1 << bit) % 2
    high = replica // (1 << top) % 2
    near = {"replica": replica + (1 - 2 * low) * (1 << bit), "tensor": tensor}
    far_step = (1 - 2 * high) * (1 << top)
    if chain:
        inner = low != high
        far = {"replica": replica + (1 - 2 * high) * (1 << bit), "tensor": tensor}
    else:
        far = {"replica": replica + far_step, "tensor": tensor}

    def peer(d):
        return lax.rem(tensor + d, n_tensor)

    feat_loads = []
    for b in range(tokens // TURN):
        block = pl.ds(b * TURN, TURN)
        feat_loads.append(pltpu.make_async_copy(feat_hbm.at[block], feat.at[block], load_sem.at[b]))
    master_load = pltpu.make_async_copy(master_hbm, master, load_sem.at[tokens // TURN])
    own_rows = pl.ds(pl.multiple_of(tensor * shard_tokens, 16), shard_tokens)
    own_grads = pltpu.make_async_copy(grad_hbm, grads.at[own_rows], load_sem.at[tokens // TURN + 1])
    for load in feat_loads:
        load.start()
    own_grads.start()
    master_load.start()

    barrier = pltpu.get_barrier_semaphore()
    for d in range(1, n_tensor):
        pl.semaphore_signal(barrier, inc=1, device_id={"replica": replica, "tensor": peer(d)}, device_id_type=MESH)
    pl.semaphore_signal(barrier, inc=1, device_id=near, device_id_type=MESH)
    if chain:
        @pl.when(inner)
        def _():
            pl.semaphore_signal(barrier, inc=1, device_id=far, device_id_type=MESH)
            pl.semaphore_wait(barrier, n_tensor + 1)

        @pl.when(jnp.logical_not(inner))
        def _():
            pl.semaphore_wait(barrier, n_tensor)
    else:
        pl.semaphore_signal(barrier, inc=1, device_id=far, device_id_type=MESH)
        pl.semaphore_wait(barrier, n_tensor + 1)

    def grad_copy(j, d, sending):
        source = tensor if sending else lax.rem(tensor + n_tensor - d, n_tensor)
        cols = pl.ds(pl.multiple_of(j * LANES, LANES), LANES)
        rows = pl.ds(pl.multiple_of(source * shard_tokens, 16), shard_tokens)
        return remote(
            grad_hbm.at[:, cols], grads.at[rows, cols], grad_send.at[j, d - 1], grad_recv.at[j, d - 1],
            {"replica": replica, "tensor": peer(d)},
        )

    def send_grads(j, carry):
        for d in range(1, n_tensor):
            grad_copy(j, d, True).start()
        return carry

    send_grads(0, 0)

    for b in range(tokens // TURN):
        feat_loads[b].wait()
        feat_t[:, b * TURN:(b + 1) * TURN] = feat[b * TURN:(b + 1) * TURN, :].T
    master_load.wait()
    working[...] = master[...].astype(jnp.bfloat16)
    own_grads.wait()
    if n_cols > 1:
        send_grads(1, 0)

    span = width if chain else width // 2
    rows = span // parts
    steps = n_cols * parts

    def place(q, half=None):
        j = q // parts
        i = q - j * parts
        start = i * rows if half is None else half * span + i * rows
        return j, pl.ds(pl.multiple_of(start, 16), rows), pl.ds(pl.multiple_of(j * LANES, LANES), LANES)

    def wait_grads(q):
        @pl.when(lax.rem(q, parts) == 0)
        def _():
            for d in range(1, n_tensor):
                grad_copy(q // parts, d, False).wait_recv()

            @pl.when(q // parts + 2 < n_cols)
            def _():
                send_grads(q // parts + 2, 0)

    def stepped(r, c):
        weight_grad = jnp.dot(feat_t[r, :], grads[:, c], preferred_element_type=jnp.float32)
        return master[r, c] - step_rate * weight_grad

    def emit(q, at, value):
        j, r, c = at
        total[j, r] = value.astype(jnp.bfloat16)
        pltpu.make_async_copy(total.at[j, r], total_hbm.at[j, r], out_sem.at[q]).start()
        remote(total.at[j, r], total_hbm.at[j, r], send_c.at[q], recv_c.at[q], near).start()

    n_blocks = 8
    block_tokens = tokens // n_blocks

    def input_copy(b):
        r = pl.ds(pl.multiple_of(b * block_tokens, 16), block_tokens)
        return pltpu.make_async_copy(rows_out.at[r], input_hbm.at[r], rows_sem.at[b])

    def input_block(b):
        r = pl.ds(pl.multiple_of(b * block_tokens, 16), block_tokens)
        rows_out[r, :] = lax.dot_general(
            grads[r, :], working[...], (((1,), (1,)), ((), ())), preferred_element_type=jnp.float32
        ).astype(jnp.bfloat16)
        input_copy(b).start()

    def input_blocks(q):
        @pl.when(q >= steps - parts)
        def _():
            for k in range(n_blocks // parts):
                input_block((q - (steps - parts)) * (n_blocks // parts) + k)

    def loop(begin, end, body):
        def run(q, carry):
            body(q)
            return carry

        lax.fori_loop(begin, end, run, 0)

    if chain:
        def to_near(q):
            j, r, c = place(q)
            return remote(outgoing.at[j, r], first_in.at[j, r], send_a.at[q], recv_a.at[q], near)

        def to_far(q):
            j, r, c = place(q)
            return remote(outgoing.at[j, r], second_in.at[j, r], send_b.at[q], recv_b.at[q], far)

        def back(q):
            j, r, c = place(q)
            return remote(total.at[j, r], total_hbm.at[j, r], send_c.at[q], recv_c.at[q], near)

        @pl.when(jnp.logical_not(inner))
        def _():
            def give(q):
                wait_grads(q)
                j, r, c = place(q)
                outgoing[j, r] = stepped(r, c).astype(jnp.bfloat16)

                @pl.when(q >= 2)
                def _():
                    to_near(q - 2).wait_send()

                to_near(q).start()
                input_blocks(q)

            loop(0, steps, give)
            loop(steps - 2, steps, lambda q: to_near(q).wait_send())
            loop(0, steps, lambda q: back(q).wait_recv())

        @pl.when(inner)
        def _():
            def finish(q):
                j, r, c = place(q)
                to_far(q).wait_recv()
                emit(q, (j, r, c), partial_sum[j, r] + second_in[j, r].astype(jnp.float32))

            def merge(q):
                wait_grads(q)
                j, r, c = place(q)
                own = stepped(r, c)
                to_near(q).wait_recv()
                own = own + first_in[j, r].astype(jnp.float32)
                partial_sum[j, r] = own
                outgoing[j, r] = own.astype(jnp.bfloat16)
                to_far(q).start()

                @pl.when(q >= lag)
                def _():
                    finish(q - lag)

                input_blocks(q)

            loop(0, steps, merge)
            loop(steps - lag, steps, finish)

            def settle(q):
                j, r, c = place(q)
                to_far(q).wait_send()
                back(q).wait_send()
                pltpu.make_async_copy(total.at[j, r], total_hbm.at[j, r], out_sem.at[q]).wait()

            loop(0, steps, settle)
    else:
        def to_near(q, half):
            j, r, c = place(q, half)
            return remote(outgoing.at[j, r], first_in.at[j, r], send_a.at[q], recv_a.at[q], near)

        def to_far(q):
            j, r, c = place(q, low)
            return remote(outgoing.at[j, r], second_in.at[j, r], send_b.at[q], recv_b.at[q], far)

        def back(q, half):
            j, r, c = place(q, half)
            return remote(total.at[j, r], total_hbm.at[j, r], send_c.at[q], recv_c.at[q], near)

        def merge(q):
            j, r, c = place(q, low)
            to_near(q, low).wait_recv()
            both = partial_sum[j, r] + first_in[j, r].astype(jnp.float32)
            partial_sum[j, r] = both
            outgoing[j, r] = both.astype(jnp.bfloat16)

            @pl.when(q >= 3)
            def _():
                to_far(q - 3).wait_send()

            to_far(q).start()

        def finish(q):
            j, r, c = place(q, low)
            to_far(q).wait_recv()
            emit(q, (j, r, c), partial_sum[j, r] + second_in[j, r].astype(jnp.float32))

        def give(q):
            wait_grads(q)
            j, r, c = place(q, 1 - low)
            outgoing[j, r] = stepped(r, c).astype(jnp.bfloat16)
            to_near(q, 1 - low).start()
            j, r, c = place(q, low)
            partial_sum[j, r] = stepped(r, c)
            merge(q)
            input_blocks(q)

            @pl.when(q >= lag)
            def _():
                finish(q - lag)

        loop(0, steps, give)
        loop(steps - lag, steps, finish)
        loop(steps - 3, steps, lambda q: to_far(q).wait_send())

        def settle(q):
            j, r, c = place(q, low)
            to_near(q, 1 - low).wait_send()
            back(q, low).wait_send()
            back(q, 1 - low).wait_recv()
            pltpu.make_async_copy(total.at[j, r], total_hbm.at[j, r], out_sem.at[q]).wait()

        loop(0, steps, settle)

    def settle_grads(j, carry):
        for d in range(1, n_tensor):
            grad_copy(j, d, True).wait_send()
        return carry

    lax.fori_loop(0, n_cols, settle_grads, 0)
    loop(0, n_blocks, lambda b: input_copy(b).wait())


def gossip(features, key_grad, shard, bit, top, n_tensor):
    tokens, width = features.shape
    columns = key_grad.shape[1]
    chain = bit == top - 1
    parts, lag = (4, 3) if chain else (2, 3)
    n_cols = columns // LANES
    steps = n_cols * parts
    dma = pltpu.SemaphoreType.DMA
    half, full = jnp.bfloat16, jnp.float32
    return pl.pallas_call(
        partial(kernel, bit, top, n_tensor, parts, lag),
        out_shape=(
            jax.ShapeDtypeStruct((n_cols, width, LANES), half),
            jax.ShapeDtypeStruct((tokens, width), half),
        ),
        in_specs=[pl.BlockSpec(memory_space=pl.ANY)] * 3,
        out_specs=[pl.BlockSpec(memory_space=pl.ANY)] * 2,
        scratch_shapes=[
            pltpu.VMEM((tokens, width), half),
            pltpu.VMEM((width, tokens), half),
            pltpu.VMEM((tokens, columns), half),
            pltpu.VMEM((width, columns), full),
            pltpu.VMEM((width, columns), half),
            pltpu.VMEM((n_cols, width, LANES), half),
            pltpu.VMEM((n_cols, width, LANES), half),
            pltpu.VMEM((n_cols, width, LANES), half),
            pltpu.VMEM((n_cols, width, LANES), full),
            pltpu.VMEM((n_cols, width, LANES), half),
            pltpu.VMEM((tokens, width), half),
            dma((tokens // TURN + 2,)),
            dma((n_cols, n_tensor - 1)),
            dma((n_cols, n_tensor - 1)),
            dma((steps,)),
            dma((8,)),
            dma((steps,)), dma((steps,)), dma((steps,)), dma((steps,)), dma((steps,)), dma((steps,)),
        ],
        compiler_params=pltpu.CompilerParams(
            collective_id=bit, has_side_effects=True, vmem_limit_bytes=36 * 1024 * 1024
        ),
        name=f"gossip_{bit}",
    )(features, key_grad, shard)


def write_outputs(pieces, total_in, input_in, master_out, working_out, input_out, total, master, working, sem):
    n_cols, width, _ = total.shape
    rows = width // pieces
    tokens = input_in.shape[0]

    def copy(k, src, dst, i):
        return pltpu.make_async_copy(src, dst, sem.at[k, i])

    loads, stores = [], []
    for i in range(pieces):
        r = pl.ds(i * rows, rows)
        loads.append(copy(0, total_in.at[:, r], total.at[:, r], i))
        loads[i].start()
    for i in range(pieces):
        r = pl.ds(i * (tokens // pieces), tokens // pieces)
        stores.append(copy(1, input_in.at[r], input_out.at[r], i))
        stores[-1].start()
    for i in range(pieces):
        r = pl.ds(i * rows, rows)
        loads[i].wait()
        for j in range(n_cols):
            mean = 0.25 * total[j, i * rows:(i + 1) * rows, :].astype(jnp.float32)
            master[i * rows:(i + 1) * rows, j * LANES:(j + 1) * LANES] = mean
            working[i * rows:(i + 1) * rows, j * LANES:(j + 1) * LANES] = mean.astype(jnp.bfloat16)
        for k, src, dst in ((2, master, master_out), (3, working, working_out)):
            stores.append(copy(k, src.at[r], dst.at[r], i))
            stores[-1].start()
    for store in stores:
        store.wait()


def outputs(total, input_rows, pieces=5):
    n_cols, width, _ = total.shape
    columns = n_cols * LANES
    half, full = jnp.bfloat16, jnp.float32
    return pl.pallas_call(
        partial(write_outputs, pieces),
        out_shape=(
            jax.ShapeDtypeStruct((width, columns), full),
            jax.ShapeDtypeStruct((width, columns), half),
            jax.ShapeDtypeStruct(input_rows.shape, half),
        ),
        in_specs=[pl.BlockSpec(memory_space=pl.ANY)] * 2,
        out_specs=[pl.BlockSpec(memory_space=pl.ANY)] * 3,
        scratch_shapes=[
            pltpu.VMEM(total.shape, half),
            pltpu.VMEM((width, columns), full),
            pltpu.VMEM((width, columns), half),
            pltpu.SemaphoreType.DMA((4, pieces)),
        ],
        compiler_params=pltpu.CompilerParams(vmem_limit_bytes=24 * 1024 * 1024),
        name="write_outputs",
    )(total, input_rows)


def solution(mesh):
    n_tensor = mesh.shape["tensor"]
    top = mesh.shape["replica"].bit_length() - 2

    def local(features, key_grad, master, exponents):
        which = jnp.minimum(exponents[0], exponents[1])
        branches = [partial(gossip, bit=bit, top=top, n_tensor=n_tensor) for bit in range(top)]
        total, input_rows = lax.switch(which, branches, features, key_grad, master[0])
        new_master, new_working, input_grad = outputs(total, input_rows)
        return new_master[None], new_working[None], input_grad

    in_specs = (
        P("replica", "tensor"),
        P(("replica", "tensor"), None),
        P("replica", "tensor", None),
        P(),
    )
    out_specs = (P("replica", "tensor", None), P("replica", "tensor", None), P("replica", "tensor"))
    return jax.shard_map(local, mesh=mesh, in_specs=in_specs, out_specs=out_specs, check_vma=False)
```

```python
from functools import partial

import jax
import jax.numpy as jnp
from jax import lax
from jax.experimental import pallas as pl
from jax.experimental.pallas import tpu as pltpu
from jax.sharding import PartitionSpec as P

MESH = pl.DeviceIdType.MESH
step_rate = 0.2
LANES = 128
TURN = 256


def remote(src, dst, send_sem, recv_sem, device):
    return pltpu.make_async_remote_copy(
        src_ref=src, dst_ref=dst, send_sem=send_sem, recv_sem=recv_sem,
        device_id=device, device_id_type=MESH,
    )


def kernel(
    bit, top, n_tensor, parts, lag, flying,
    feat_hbm, grad_hbm, master_hbm,
    total_hbm, input_hbm,
    feat, feat_t, grads, master, working, outgoing, first_in, second_in, partial_sum, total, rows_out,
    load_sem, grad_send, grad_recv, out_sem, rows_sem,
    send_a, recv_a, send_b, recv_b, send_c, recv_c,
):
    replica, tensor = lax.axis_index("replica"), lax.axis_index("tensor")
    tokens, width = feat.shape
    columns = grads.shape[1]
    shard_tokens = grad_hbm.shape[0]
    n_cols = columns // LANES
    chain = bit == top - 1
    low = replica // (1 << bit) % 2
    high = replica // (1 << top) % 2
    near = {"replica": replica + (1 - 2 * low) * (1 << bit), "tensor": tensor}
    far_step = (1 - 2 * high) * (1 << top)
    if chain:
        inner = low != high
        far = {"replica": replica + (1 - 2 * high) * (1 << bit), "tensor": tensor}
    else:
        far = {"replica": replica + far_step, "tensor": tensor}

    def peer(d):
        return lax.rem(tensor + d, n_tensor)

    feat_loads = []
    for b in range(tokens // TURN):
        block = pl.ds(b * TURN, TURN)
        feat_loads.append(pltpu.make_async_copy(feat_hbm.at[block], feat.at[block], load_sem.at[b]))
    master_load = pltpu.make_async_copy(master_hbm, master, load_sem.at[tokens // TURN])
    own_rows = pl.ds(pl.multiple_of(tensor * shard_tokens, 16), shard_tokens)
    own_grads = pltpu.make_async_copy(grad_hbm, grads.at[own_rows], load_sem.at[tokens // TURN + 1])
    for load in feat_loads:
        load.start()
    own_grads.start()
    master_load.start()

    barrier = pltpu.get_barrier_semaphore()
    for d in range(1, n_tensor):
        pl.semaphore_signal(barrier, inc=1, device_id={"replica": replica, "tensor": peer(d)}, device_id_type=MESH)
    pl.semaphore_signal(barrier, inc=1, device_id=near, device_id_type=MESH)
    if chain:
        @pl.when(inner)
        def _():
            pl.semaphore_signal(barrier, inc=1, device_id=far, device_id_type=MESH)
            pl.semaphore_wait(barrier, n_tensor + 1)

        @pl.when(jnp.logical_not(inner))
        def _():
            pl.semaphore_wait(barrier, n_tensor)
    else:
        pl.semaphore_signal(barrier, inc=1, device_id=far, device_id_type=MESH)
        pl.semaphore_wait(barrier, n_tensor + 1)

    def grad_copy(j, d, sending):
        source = tensor if sending else lax.rem(tensor + n_tensor - d, n_tensor)
        cols = pl.ds(pl.multiple_of(j * LANES, LANES), LANES)
        rows = pl.ds(pl.multiple_of(source * shard_tokens, 16), shard_tokens)
        return remote(
            grad_hbm.at[:, cols], grads.at[rows, cols], grad_send.at[j, d - 1], grad_recv.at[j, d - 1],
            {"replica": replica, "tensor": peer(d)},
        )

    def send_grads(j, carry):
        for d in range(1, n_tensor):
            grad_copy(j, d, True).start()
        return carry

    send_grads(0, 0)

    for b in range(tokens // TURN):
        feat_loads[b].wait()
        feat_t[:, b * TURN:(b + 1) * TURN] = feat[b * TURN:(b + 1) * TURN, :].T
    master_load.wait()
    working[...] = master[...].astype(jnp.bfloat16)
    own_grads.wait()
    if n_cols > 1:
        send_grads(1, 0)

    span = width if chain else width // 2
    rows = span // parts
    steps = n_cols * parts

    def place(q, half=None):
        j = q // parts
        i = q - j * parts
        start = i * rows if half is None else half * span + i * rows
        return j, pl.ds(pl.multiple_of(start, 16), rows), pl.ds(pl.multiple_of(j * LANES, LANES), LANES)

    def wait_grads(q):
        @pl.when(lax.rem(q, parts) == 0)
        def _():
            for d in range(1, n_tensor):
                grad_copy(q // parts, d, False).wait_recv()

            @pl.when(q // parts + 2 < n_cols)
            def _():
                send_grads(q // parts + 2, 0)

    def stepped(r, c):
        weight_grad = jnp.dot(feat_t[r, :], grads[:, c], preferred_element_type=jnp.float32)
        return master[r, c] - step_rate * weight_grad

    def emit(q, at, value):
        j, r, c = at
        total[j, r] = value.astype(jnp.bfloat16)
        pltpu.make_async_copy(total.at[j, r], total_hbm.at[j, r], out_sem.at[q]).start()
        remote(total.at[j, r], total_hbm.at[j, r], send_c.at[q], recv_c.at[q], near).start()

    n_blocks = 8
    block_tokens = tokens // n_blocks

    def input_copy(b):
        r = pl.ds(pl.multiple_of(b * block_tokens, 16), block_tokens)
        return pltpu.make_async_copy(rows_out.at[r], input_hbm.at[r], rows_sem.at[b])

    def input_block(b):
        r = pl.ds(pl.multiple_of(b * block_tokens, 16), block_tokens)
        rows_out[r, :] = lax.dot_general(
            grads[r, :], working[...], (((1,), (1,)), ((), ())), preferred_element_type=jnp.float32
        ).astype(jnp.bfloat16)
        input_copy(b).start()

    def input_blocks(q):
        @pl.when(q >= steps - parts)
        def _():
            for k in range(n_blocks // parts):
                input_block((q - (steps - parts)) * (n_blocks // parts) + k)

    def loop(begin, end, body):
        def run(q, carry):
            body(q)
            return carry

        lax.fori_loop(begin, end, run, 0)

    if chain:
        def to_near(q):
            j, r, c = place(q)
            return remote(outgoing.at[j, r], first_in.at[j, r], send_a.at[q], recv_a.at[q], near)

        def to_far(q):
            j, r, c = place(q)
            return remote(outgoing.at[j, r], second_in.at[j, r], send_b.at[q], recv_b.at[q], far)

        def back(q):
            j, r, c = place(q)
            return remote(total.at[j, r], total_hbm.at[j, r], send_c.at[q], recv_c.at[q], near)

        @pl.when(jnp.logical_not(inner))
        def _():
            def give(q):
                wait_grads(q)
                j, r, c = place(q)
                outgoing[j, r] = stepped(r, c).astype(jnp.bfloat16)

                @pl.when(q >= flying)
                def _():
                    to_near(q - flying).wait_send()

                to_near(q).start()
                input_blocks(q)

            loop(0, steps, give)
            loop(steps - flying, steps, lambda q: to_near(q).wait_send())
            loop(0, steps, lambda q: back(q).wait_recv())

        @pl.when(inner)
        def _():
            def finish(q):
                j, r, c = place(q)
                to_far(q).wait_recv()
                emit(q, (j, r, c), partial_sum[j, r] + second_in[j, r].astype(jnp.float32))

            def merge(q):
                wait_grads(q)
                j, r, c = place(q)
                own = stepped(r, c)
                to_near(q).wait_recv()
                own = own + first_in[j, r].astype(jnp.float32)
                partial_sum[j, r] = own
                outgoing[j, r] = own.astype(jnp.bfloat16)
                to_far(q).start()

                @pl.when(q >= lag)
                def _():
                    finish(q - lag)

                input_blocks(q)

            loop(0, steps, merge)
            loop(steps - lag, steps, finish)

            def settle(q):
                j, r, c = place(q)
                to_far(q).wait_send()
                back(q).wait_send()
                pltpu.make_async_copy(total.at[j, r], total_hbm.at[j, r], out_sem.at[q]).wait()

            loop(0, steps, settle)
    else:
        def to_near(q, half):
            j, r, c = place(q, half)
            return remote(outgoing.at[j, r], first_in.at[j, r], send_a.at[q], recv_a.at[q], near)

        def to_far(q):
            j, r, c = place(q, low)
            return remote(outgoing.at[j, r], second_in.at[j, r], send_b.at[q], recv_b.at[q], far)

        def back(q, half):
            j, r, c = place(q, half)
            return remote(total.at[j, r], total_hbm.at[j, r], send_c.at[q], recv_c.at[q], near)

        def merge(q):
            j, r, c = place(q, low)
            to_near(q, low).wait_recv()
            both = partial_sum[j, r] + first_in[j, r].astype(jnp.float32)
            partial_sum[j, r] = both
            outgoing[j, r] = both.astype(jnp.bfloat16)

            @pl.when(q >= flying)
            def _():
                to_far(q - flying).wait_send()

            to_far(q).start()

        def finish(q):
            j, r, c = place(q, low)
            to_far(q).wait_recv()
            emit(q, (j, r, c), partial_sum[j, r] + second_in[j, r].astype(jnp.float32))

        def give(q):
            wait_grads(q)
            j, r, c = place(q, 1 - low)
            outgoing[j, r] = stepped(r, c).astype(jnp.bfloat16)
            to_near(q, 1 - low).start()
            j, r, c = place(q, low)
            partial_sum[j, r] = stepped(r, c)
            merge(q)
            input_blocks(q)

            @pl.when(q >= lag)
            def _():
                finish(q - lag)

        loop(0, steps, give)
        loop(steps - lag, steps, finish)
        loop(steps - flying, steps, lambda q: to_far(q).wait_send())

        def settle(q):
            j, r, c = place(q, low)
            to_near(q, 1 - low).wait_send()
            back(q, low).wait_send()
            back(q, 1 - low).wait_recv()
            pltpu.make_async_copy(total.at[j, r], total_hbm.at[j, r], out_sem.at[q]).wait()

        loop(0, steps, settle)

    def settle_grads(j, carry):
        for d in range(1, n_tensor):
            grad_copy(j, d, True).wait_send()
        return carry

    lax.fori_loop(0, n_cols, settle_grads, 0)
    loop(0, n_blocks, lambda b: input_copy(b).wait())


def gossip(features, key_grad, shard, bit, top, n_tensor):
    tokens, width = features.shape
    columns = key_grad.shape[1]
    chain = bit == top - 1
    span = width if chain else width // 2
    parts, lag, flying = (8, 3, 4) if chain else (4, 4, 3)
    if span // parts % 16:
        parts //= 2
    n_cols = columns // LANES
    steps = n_cols * parts
    dma = pltpu.SemaphoreType.DMA
    half, full = jnp.bfloat16, jnp.float32
    return pl.pallas_call(
        partial(kernel, bit, top, n_tensor, parts, lag, flying),
        out_shape=(
            jax.ShapeDtypeStruct((n_cols, width, LANES), half),
            jax.ShapeDtypeStruct((tokens, width), half),
        ),
        in_specs=[pl.BlockSpec(memory_space=pl.ANY)] * 3,
        out_specs=[pl.BlockSpec(memory_space=pl.ANY)] * 2,
        scratch_shapes=[
            pltpu.VMEM((tokens, width), half),
            pltpu.VMEM((width, tokens), half),
            pltpu.VMEM((tokens, columns), half),
            pltpu.VMEM((width, columns), full),
            pltpu.VMEM((width, columns), half),
            pltpu.VMEM((n_cols, width, LANES), half),
            pltpu.VMEM((n_cols, width, LANES), half),
            pltpu.VMEM((n_cols, width, LANES), half),
            pltpu.VMEM((n_cols, width, LANES), full),
            pltpu.VMEM((n_cols, width, LANES), half),
            pltpu.VMEM((tokens, width), half),
            dma((tokens // TURN + 2,)),
            dma((n_cols, n_tensor - 1)),
            dma((n_cols, n_tensor - 1)),
            dma((steps,)),
            dma((8,)),
            dma((steps,)), dma((steps,)), dma((steps,)), dma((steps,)), dma((steps,)), dma((steps,)),
        ],
        compiler_params=pltpu.CompilerParams(
            collective_id=bit, has_side_effects=True, vmem_limit_bytes=36 * 1024 * 1024
        ),
        name=f"gossip_{bit}",
    )(features, key_grad, shard)


def write_outputs(pieces, total_in, input_in, master_out, working_out, input_out, total, master, working, sem):
    n_cols, width, _ = total.shape
    rows = width // pieces
    tokens = input_in.shape[0]

    def copy(k, src, dst, i):
        return pltpu.make_async_copy(src, dst, sem.at[k, i])

    loads, stores = [], []
    for i in range(pieces):
        r = pl.ds(i * rows, rows)
        loads.append(copy(0, total_in.at[:, r], total.at[:, r], i))
        loads[i].start()
    for i in range(pieces):
        r = pl.ds(i * (tokens // pieces), tokens // pieces)
        stores.append(copy(1, input_in.at[r], input_out.at[r], i))
        stores[-1].start()
    for i in range(pieces):
        r = pl.ds(i * rows, rows)
        loads[i].wait()
        for j in range(n_cols):
            mean = 0.25 * total[j, i * rows:(i + 1) * rows, :].astype(jnp.float32)
            master[i * rows:(i + 1) * rows, j * LANES:(j + 1) * LANES] = mean
            working[i * rows:(i + 1) * rows, j * LANES:(j + 1) * LANES] = mean.astype(jnp.bfloat16)
        for k, src, dst in ((2, master, master_out), (3, working, working_out)):
            stores.append(copy(k, src.at[r], dst.at[r], i))
            stores[-1].start()
    for store in stores:
        store.wait()


def outputs(total, input_rows, pieces=5):
    n_cols, width, _ = total.shape
    columns = n_cols * LANES
    half, full = jnp.bfloat16, jnp.float32
    return pl.pallas_call(
        partial(write_outputs, pieces),
        out_shape=(
            jax.ShapeDtypeStruct((width, columns), full),
            jax.ShapeDtypeStruct((width, columns), half),
            jax.ShapeDtypeStruct(input_rows.shape, half),
        ),
        in_specs=[pl.BlockSpec(memory_space=pl.ANY)] * 2,
        out_specs=[pl.BlockSpec(memory_space=pl.ANY)] * 3,
        scratch_shapes=[
            pltpu.VMEM(total.shape, half),
            pltpu.VMEM((width, columns), full),
            pltpu.VMEM((width, columns), half),
            pltpu.SemaphoreType.DMA((4, pieces)),
        ],
        compiler_params=pltpu.CompilerParams(vmem_limit_bytes=24 * 1024 * 1024),
        name="write_outputs",
    )(total, input_rows)


def solution(mesh):
    n_tensor = mesh.shape["tensor"]
    top = mesh.shape["replica"].bit_length() - 2

    def local(features, key_grad, master, exponents):
        which = jnp.min(exponents)
        branches = [partial(gossip, bit=bit, top=top, n_tensor=n_tensor) for bit in range(top)]
        total, input_rows = lax.switch(which, branches, features, key_grad, master[0])
        new_master, new_working, input_grad = outputs(total, input_rows)
        return new_master[None], new_working[None], input_grad

    in_specs = (
        P("replica", "tensor"),
        P(("replica", "tensor"), None),
        P("replica", "tensor", None),
        P(),
    )
    out_specs = (P("replica", "tensor", None), P("replica", "tensor", None), P("replica", "tensor"))
    return jax.shard_map(local, mesh=mesh, in_specs=in_specs, out_specs=out_specs, check_vma=False)
```

```python
from functools import partial

import jax
import jax.numpy as jnp
from jax import lax
from jax.experimental import pallas as pl
from jax.experimental.pallas import tpu as pltpu
from jax.sharding import PartitionSpec as P

MESH = pl.DeviceIdType.MESH
step_rate = 0.2
LANES = 128
TURN = 256


def remote(src, dst, send_sem, recv_sem, device):
    return pltpu.make_async_remote_copy(
        src_ref=src, dst_ref=dst, send_sem=send_sem, recv_sem=recv_sem,
        device_id=device, device_id_type=MESH,
    )


def kernel(
    bit, top, n_tensor, parts, lag,
    feat_hbm, grad_hbm, master_hbm,
    total_hbm, input_hbm,
    feat, feat_t, grads, master, working, outgoing, first_in, second_in, partial_sum, total, rows_out,
    load_sem, grad_send, grad_recv, out_sem, rows_sem,
    send_a, recv_a, send_b, recv_b, send_c, recv_c,
):
    replica, tensor = lax.axis_index("replica"), lax.axis_index("tensor")
    tokens, width = feat.shape
    columns = grads.shape[1]
    shard_tokens = grad_hbm.shape[0]
    n_cols = columns // LANES
    chain = bit == top - 1
    low = replica // (1 << bit) % 2
    high = replica // (1 << top) % 2
    near = {"replica": replica + (1 - 2 * low) * (1 << bit), "tensor": tensor}
    far_step = (1 - 2 * high) * (1 << top)
    if chain:
        inner = low != high
        far = {"replica": replica + (1 - 2 * high) * (1 << bit), "tensor": tensor}
    else:
        far = {"replica": replica + far_step, "tensor": tensor}

    def peer(d):
        return lax.rem(tensor + d, n_tensor)

    feat_loads = []
    for b in range(tokens // TURN):
        block = pl.ds(b * TURN, TURN)
        feat_loads.append(pltpu.make_async_copy(feat_hbm.at[block], feat.at[block], load_sem.at[b]))
    master_load = pltpu.make_async_copy(master_hbm, master, load_sem.at[tokens // TURN])
    own_rows = pl.ds(pl.multiple_of(tensor * shard_tokens, 16), shard_tokens)
    own_grads = pltpu.make_async_copy(grad_hbm, grads.at[own_rows], load_sem.at[tokens // TURN + 1])
    for load in feat_loads:
        load.start()
    own_grads.start()
    master_load.start()

    barrier = pltpu.get_barrier_semaphore()
    for d in range(1, n_tensor):
        pl.semaphore_signal(barrier, inc=1, device_id={"replica": replica, "tensor": peer(d)}, device_id_type=MESH)
    pl.semaphore_signal(barrier, inc=1, device_id=near, device_id_type=MESH)
    if chain:
        @pl.when(inner)
        def _():
            pl.semaphore_signal(barrier, inc=1, device_id=far, device_id_type=MESH)
            pl.semaphore_wait(barrier, n_tensor + 1)

        @pl.when(jnp.logical_not(inner))
        def _():
            pl.semaphore_wait(barrier, n_tensor)
    else:
        pl.semaphore_signal(barrier, inc=1, device_id=far, device_id_type=MESH)
        pl.semaphore_wait(barrier, n_tensor + 1)

    def grad_copy(j, d, sending):
        source = tensor if sending else lax.rem(tensor + n_tensor - d, n_tensor)
        cols = pl.ds(pl.multiple_of(j * LANES, LANES), LANES)
        rows = pl.ds(pl.multiple_of(source * shard_tokens, 16), shard_tokens)
        return remote(
            grad_hbm.at[:, cols], grads.at[rows, cols], grad_send.at[j, d - 1], grad_recv.at[j, d - 1],
            {"replica": replica, "tensor": peer(d)},
        )

    def send_grads(j, carry):
        for d in range(1, n_tensor):
            grad_copy(j, d, True).start()
        return carry

    send_grads(0, 0)

    for b in range(tokens // TURN):
        feat_loads[b].wait()
        feat_t[:, b * TURN:(b + 1) * TURN] = feat[b * TURN:(b + 1) * TURN, :].T
    master_load.wait()
    working[...] = master[...].astype(jnp.bfloat16)
    own_grads.wait()
    if n_cols > 1:
        send_grads(1, 0)

    span = width if chain else width // 2
    rows = span // parts
    steps = n_cols * parts

    def place(q, half=None):
        j = q // parts
        i = q - j * parts
        start = i * rows if half is None else half * span + i * rows
        return j, pl.ds(pl.multiple_of(start, 16), rows), pl.ds(pl.multiple_of(j * LANES, LANES), LANES)

    def wait_grads(q):
        @pl.when(lax.rem(q, parts) == 0)
        def _():
            for d in range(1, n_tensor):
                grad_copy(q // parts, d, False).wait_recv()

            @pl.when(q // parts + 2 < n_cols)
            def _():
                send_grads(q // parts + 2, 0)

    def stepped(r, c):
        weight_grad = jnp.dot(feat_t[r, :], grads[:, c], preferred_element_type=jnp.float32)
        return master[r, c] - step_rate * weight_grad

    def emit(q, at, value):
        j, r, c = at
        total[j, r] = value.astype(jnp.bfloat16)
        pltpu.make_async_copy(total.at[j, r], total_hbm.at[j, r], out_sem.at[q]).start()
        remote(total.at[j, r], total_hbm.at[j, r], send_c.at[q], recv_c.at[q], near).start()

    n_blocks = 8
    block_tokens = tokens // n_blocks

    def input_copy(b):
        r = pl.ds(pl.multiple_of(b * block_tokens, 16), block_tokens)
        return pltpu.make_async_copy(rows_out.at[r], input_hbm.at[r], rows_sem.at[b])

    def input_block(b):
        r = pl.ds(pl.multiple_of(b * block_tokens, 16), block_tokens)
        rows_out[r, :] = lax.dot_general(
            grads[r, :], working[...], (((1,), (1,)), ((), ())), preferred_element_type=jnp.float32
        ).astype(jnp.bfloat16)
        input_copy(b).start()

    def input_blocks(q):
        @pl.when(q >= steps - parts)
        def _():
            for k in range(n_blocks // parts):
                input_block((q - (steps - parts)) * (n_blocks // parts) + k)

    def loop(begin, end, body):
        def run(q, carry):
            body(q)
            return carry

        lax.fori_loop(begin, end, run, 0)

    if chain:
        def to_near(q):
            j, r, c = place(q)
            return remote(outgoing.at[j, r], first_in.at[j, r], send_a.at[q], recv_a.at[q], near)

        def to_far(q):
            j, r, c = place(q)
            return remote(outgoing.at[j, r], second_in.at[j, r], send_b.at[q], recv_b.at[q], far)

        def back(q):
            j, r, c = place(q)
            return remote(total.at[j, r], total_hbm.at[j, r], send_c.at[q], recv_c.at[q], near)

        @pl.when(jnp.logical_not(inner))
        def _():
            def give(q):
                wait_grads(q)
                j, r, c = place(q)
                outgoing[j, r] = stepped(r, c).astype(jnp.bfloat16)

                to_near(q).start()
                input_blocks(q)

            loop(0, steps, give)
            loop(0, steps, lambda q: to_near(q).wait_send())
            loop(0, steps, lambda q: back(q).wait_recv())

        @pl.when(inner)
        def _():
            def finish(q):
                j, r, c = place(q)
                to_far(q).wait_recv()
                emit(q, (j, r, c), partial_sum[j, r] + second_in[j, r].astype(jnp.float32))

            def merge(q):
                wait_grads(q)
                j, r, c = place(q)
                own = stepped(r, c)
                to_near(q).wait_recv()
                own = own + first_in[j, r].astype(jnp.float32)
                partial_sum[j, r] = own
                outgoing[j, r] = own.astype(jnp.bfloat16)
                to_far(q).start()

                @pl.when(q >= lag)
                def _():
                    finish(q - lag)

                input_blocks(q)

            loop(0, steps, merge)
            loop(steps - lag, steps, finish)

            def settle(q):
                j, r, c = place(q)
                to_far(q).wait_send()
                back(q).wait_send()
                pltpu.make_async_copy(total.at[j, r], total_hbm.at[j, r], out_sem.at[q]).wait()

            loop(0, steps, settle)
    else:
        def to_near(q, half):
            j, r, c = place(q, half)
            return remote(outgoing.at[j, r], first_in.at[j, r], send_a.at[q], recv_a.at[q], near)

        def to_far(q):
            j, r, c = place(q, low)
            return remote(outgoing.at[j, r], second_in.at[j, r], send_b.at[q], recv_b.at[q], far)

        def back(q, half):
            j, r, c = place(q, half)
            return remote(total.at[j, r], total_hbm.at[j, r], send_c.at[q], recv_c.at[q], near)

        def merge(q):
            j, r, c = place(q, low)
            to_near(q, low).wait_recv()
            both = partial_sum[j, r] + first_in[j, r].astype(jnp.float32)
            partial_sum[j, r] = both
            outgoing[j, r] = both.astype(jnp.bfloat16)
            to_far(q).start()

        def finish(q):
            j, r, c = place(q, low)
            to_far(q).wait_recv()
            emit(q, (j, r, c), partial_sum[j, r] + second_in[j, r].astype(jnp.float32))

        def give(q):
            wait_grads(q)
            j, r, c = place(q, 1 - low)
            outgoing[j, r] = stepped(r, c).astype(jnp.bfloat16)
            to_near(q, 1 - low).start()
            j, r, c = place(q, low)
            partial_sum[j, r] = stepped(r, c)
            merge(q)
            input_blocks(q)

        loop(0, steps, give)
        loop(0, steps, finish)
        loop(0, steps, lambda q: to_far(q).wait_send())

        def settle(q):
            j, r, c = place(q, low)
            to_near(q, 1 - low).wait_send()
            back(q, low).wait_send()
            back(q, 1 - low).wait_recv()
            pltpu.make_async_copy(total.at[j, r], total_hbm.at[j, r], out_sem.at[q]).wait()

        loop(0, steps, settle)

    def settle_grads(j, carry):
        for d in range(1, n_tensor):
            grad_copy(j, d, True).wait_send()
        return carry

    lax.fori_loop(0, n_cols, settle_grads, 0)
    loop(0, n_blocks, lambda b: input_copy(b).wait())


def gossip(features, key_grad, shard, bit, top, n_tensor):
    tokens, width = features.shape
    columns = key_grad.shape[1]
    chain = bit == top - 1
    span = width if chain else width // 2
    parts, lag = (8, 3) if chain else (2, 0)
    if span // parts % 16:
        parts //= 2
    n_cols = columns // LANES
    steps = n_cols * parts
    dma = pltpu.SemaphoreType.DMA
    half, full = jnp.bfloat16, jnp.float32
    return pl.pallas_call(
        partial(kernel, bit, top, n_tensor, parts, lag),
        out_shape=(
            jax.ShapeDtypeStruct((n_cols, width, LANES), half),
            jax.ShapeDtypeStruct((tokens, width), half),
        ),
        in_specs=[pl.BlockSpec(memory_space=pl.ANY)] * 3,
        out_specs=[pl.BlockSpec(memory_space=pl.ANY)] * 2,
        scratch_shapes=[
            pltpu.VMEM((tokens, width), half),
            pltpu.VMEM((width, tokens), half),
            pltpu.VMEM((tokens, columns), half),
            pltpu.VMEM((width, columns), full),
            pltpu.VMEM((width, columns), half),
            pltpu.VMEM((n_cols, width, LANES), half),
            pltpu.VMEM((n_cols, width, LANES), half),
            pltpu.VMEM((n_cols, width, LANES), half),
            pltpu.VMEM((n_cols, width, LANES), full),
            pltpu.VMEM((n_cols, width, LANES), half),
            pltpu.VMEM((tokens, width), half),
            dma((tokens // TURN + 2,)),
            dma((n_cols, n_tensor - 1)),
            dma((n_cols, n_tensor - 1)),
            dma((steps,)),
            dma((8,)),
            dma((steps,)), dma((steps,)), dma((steps,)), dma((steps,)), dma((steps,)), dma((steps,)),
        ],
        compiler_params=pltpu.CompilerParams(
            collective_id=bit, has_side_effects=True, vmem_limit_bytes=36 * 1024 * 1024
        ),
        name=f"gossip_{bit}",
    )(features, key_grad, shard)


def write_outputs(pieces, total_in, input_in, master_out, working_out, input_out, total, master, working, sem):
    n_cols, width, _ = total.shape
    rows = width // pieces
    tokens = input_in.shape[0]

    def copy(k, src, dst, i):
        return pltpu.make_async_copy(src, dst, sem.at[k, i])

    loads, stores = [], []
    for i in range(pieces):
        r = pl.ds(i * rows, rows)
        loads.append(copy(0, total_in.at[:, r], total.at[:, r], i))
        loads[i].start()
    for i in range(pieces):
        r = pl.ds(i * (tokens // pieces), tokens // pieces)
        stores.append(copy(1, input_in.at[r], input_out.at[r], i))
        stores[-1].start()
    for i in range(pieces):
        r = pl.ds(i * rows, rows)
        loads[i].wait()
        for j in range(n_cols):
            mean = 0.25 * total[j, i * rows:(i + 1) * rows, :].astype(jnp.float32)
            master[i * rows:(i + 1) * rows, j * LANES:(j + 1) * LANES] = mean
            working[i * rows:(i + 1) * rows, j * LANES:(j + 1) * LANES] = mean.astype(jnp.bfloat16)
        for k, src, dst in ((2, master, master_out), (3, working, working_out)):
            stores.append(copy(k, src.at[r], dst.at[r], i))
            stores[-1].start()
    for store in stores:
        store.wait()


def outputs(total, input_rows, pieces=5):
    n_cols, width, _ = total.shape
    columns = n_cols * LANES
    half, full = jnp.bfloat16, jnp.float32
    return pl.pallas_call(
        partial(write_outputs, pieces),
        out_shape=(
            jax.ShapeDtypeStruct((width, columns), full),
            jax.ShapeDtypeStruct((width, columns), half),
            jax.ShapeDtypeStruct(input_rows.shape, half),
        ),
        in_specs=[pl.BlockSpec(memory_space=pl.ANY)] * 2,
        out_specs=[pl.BlockSpec(memory_space=pl.ANY)] * 3,
        scratch_shapes=[
            pltpu.VMEM(total.shape, half),
            pltpu.VMEM((width, columns), full),
            pltpu.VMEM((width, columns), half),
            pltpu.SemaphoreType.DMA((4, pieces)),
        ],
        compiler_params=pltpu.CompilerParams(vmem_limit_bytes=24 * 1024 * 1024),
        name="write_outputs",
    )(total, input_rows)


def solution(mesh):
    n_tensor = mesh.shape["tensor"]
    top = mesh.shape["replica"].bit_length() - 2

    def local(features, key_grad, master, exponents):
        which = jnp.min(exponents)
        branches = [partial(gossip, bit=bit, top=top, n_tensor=n_tensor) for bit in range(top)]
        total, input_rows = lax.switch(which, branches, features, key_grad, master[0])
        new_master, new_working, input_grad = outputs(total, input_rows)
        return new_master[None], new_working[None], input_grad

    in_specs = (
        P("replica", "tensor"),
        P(("replica", "tensor"), None),
        P("replica", "tensor", None),
        P(),
    )
    out_specs = (P("replica", "tensor", None), P("replica", "tensor", None), P("replica", "tensor"))
    return jax.shard_map(local, mesh=mesh, in_specs=in_specs, out_specs=out_specs, check_vma=False)
```

```python
from functools import partial

import jax
import jax.numpy as jnp
from jax import lax
from jax.experimental import pallas as pl
from jax.experimental.pallas import tpu as pltpu
from jax.sharding import PartitionSpec as P

MESH = pl.DeviceIdType.MESH
step_rate = 0.2
LANES = 128
LOADS = 5


def remote(src, dst, send_sem, recv_sem, device):
    return pltpu.make_async_remote_copy(
        src_ref=src, dst_ref=dst, send_sem=send_sem, recv_sem=recv_sem,
        device_id=device, device_id_type=MESH,
    )


def kernel(
    bit, top, n_tensor, parts, lag,
    feat_hbm, grad_hbm, master_hbm,
    total_hbm, input_hbm,
    feat, grads_t, grads, master, working, outgoing, first_in, second_in, stepped, total, rows_out,
    load_sem, grad_send, grad_recv, out_sem, rows_sem,
    send_a, recv_a, send_b, recv_b, send_c, recv_c,
):
    replica, tensor = lax.axis_index("replica"), lax.axis_index("tensor")
    tokens, width = feat.shape
    columns = grads.shape[1]
    shard_tokens = grad_hbm.shape[0]
    n_cols = columns // LANES
    chain = bit == top - 1
    low = replica // (1 << bit) % 2
    high = replica // (1 << top) % 2
    near = {"replica": replica + (1 - 2 * low) * (1 << bit), "tensor": tensor}
    far_step = (1 - 2 * high) * (1 << top)
    if chain:
        inner = low != high
        far = {"replica": replica + (1 - 2 * high) * (1 << bit), "tensor": tensor}
    else:
        far = {"replica": replica + far_step, "tensor": tensor}

    def peer(d):
        return lax.rem(tensor + d, n_tensor)

    feat_loads = []
    for b in range(LOADS):
        block = pl.ds(b * (tokens // LOADS), tokens // LOADS)
        feat_loads.append(pltpu.make_async_copy(feat_hbm.at[block], feat.at[block], load_sem.at[b]))
    master_load = pltpu.make_async_copy(master_hbm, master, load_sem.at[LOADS])
    own_rows = pl.ds(pl.multiple_of(tensor * shard_tokens, 16), shard_tokens)
    own_grads = pltpu.make_async_copy(grad_hbm, grads.at[own_rows], load_sem.at[LOADS + 1])
    for load in feat_loads:
        load.start()
    own_grads.start()
    master_load.start()

    barrier = pltpu.get_barrier_semaphore()
    for d in range(1, n_tensor):
        pl.semaphore_signal(barrier, inc=1, device_id={"replica": replica, "tensor": peer(d)}, device_id_type=MESH)
    pl.semaphore_signal(barrier, inc=1, device_id=near, device_id_type=MESH)
    if chain:
        @pl.when(inner)
        def _():
            pl.semaphore_signal(barrier, inc=1, device_id=far, device_id_type=MESH)
            pl.semaphore_wait(barrier, n_tensor + 1)

        @pl.when(jnp.logical_not(inner))
        def _():
            pl.semaphore_wait(barrier, n_tensor)
    else:
        pl.semaphore_signal(barrier, inc=1, device_id=far, device_id_type=MESH)
        pl.semaphore_wait(barrier, n_tensor + 1)

    def grad_copy(j, d, sending):
        source = tensor if sending else lax.rem(tensor + n_tensor - d, n_tensor)
        cols = pl.ds(pl.multiple_of(j * LANES, LANES), LANES)
        rows = pl.ds(pl.multiple_of(source * shard_tokens, 16), shard_tokens)
        return remote(
            grad_hbm.at[:, cols], grads.at[rows, cols], grad_send.at[j, d - 1], grad_recv.at[j, d - 1],
            {"replica": replica, "tensor": peer(d)},
        )

    def send_grads(j, carry):
        for d in range(1, n_tensor):
            grad_copy(j, d, True).start()
        return carry

    send_grads(0, 0)

    for load in feat_loads:
        load.wait()
    own_grads.wait()
    master_load.wait()

    span = width if chain else width // 2
    rows = span // parts
    steps = n_cols * parts

    def place(q, half=None):
        j = q // parts
        i = q - j * parts
        start = i * rows if half is None else half * span + i * rows
        return j, pl.ds(pl.multiple_of(start, 16), rows), pl.ds(pl.multiple_of(j * LANES, LANES), LANES)

    def take_grads(j):
        for d in range(1, n_tensor):
            grad_copy(j, d, False).wait_recv()

        @pl.when(j + 1 < n_cols)
        def _():
            send_grads(j + 1, 0)

        c = pl.ds(pl.multiple_of(j * LANES, LANES), LANES)
        grads_t[...] = grads[:, c].T

    halves = 2 if width % (2 * LANES) == 0 else 1

    def step_half(j, half):
        size = width // halves
        r = pl.ds(pl.multiple_of(half * size, LANES), size) if halves == 2 else slice(None)
        c = pl.ds(pl.multiple_of(j * LANES, LANES), LANES)
        turned = jnp.dot(grads_t[...], feat[:, r], preferred_element_type=jnp.float32)
        stepped[j, r] = master[r, c] - step_rate * turned.T

    def round_master(j):
        c = pl.ds(pl.multiple_of(j * LANES, LANES), LANES)
        working[:, c] = master[:, c].astype(jnp.bfloat16)

    def begin(q):
        j = q // parts

        @pl.when(lax.rem(q, parts) == 0)
        def _():
            take_grads(j)
            round_master(j)
            step_half(j, 0)

        if halves == 2:
            @pl.when(lax.rem(q, parts) == parts // 2)
            def _():
                step_half(j, 1)

    def emit(q, at, value):
        j, r, c = at
        total[j, r] = value.astype(jnp.bfloat16)
        pltpu.make_async_copy(total.at[j, r], total_hbm.at[j, r], out_sem.at[q]).start()
        remote(total.at[j, r], total_hbm.at[j, r], send_c.at[q], recv_c.at[q], near).start()

    n_blocks = 8
    block_tokens = tokens // n_blocks

    def input_copy(b):
        r = pl.ds(pl.multiple_of(b * block_tokens, 16), block_tokens)
        return pltpu.make_async_copy(rows_out.at[r], input_hbm.at[r], rows_sem.at[b])

    def input_block(b):
        r = pl.ds(pl.multiple_of(b * block_tokens, 16), block_tokens)
        rows_out[r, :] = lax.dot_general(
            grads[r, :], working[...], (((1,), (1,)), ((), ())), preferred_element_type=jnp.float32
        ).astype(jnp.bfloat16)
        input_copy(b).start()

    def input_blocks(q):
        @pl.when(q >= steps - parts)
        def _():
            for k in range(n_blocks // parts):
                input_block((q - (steps - parts)) * (n_blocks // parts) + k)

    def loop(begin, end, body):
        def run(q, carry):
            body(q)
            return carry

        lax.fori_loop(begin, end, run, 0)

    if chain:
        def to_near(q):
            j, r, c = place(q)
            return remote(outgoing.at[j, r], first_in.at[j, r], send_a.at[q], recv_a.at[q], near)

        def to_far(q):
            j, r, c = place(q)
            return remote(outgoing.at[j, r], second_in.at[j, r], send_b.at[q], recv_b.at[q], far)

        def back(q):
            j, r, c = place(q)
            return remote(total.at[j, r], total_hbm.at[j, r], send_c.at[q], recv_c.at[q], near)

        @pl.when(jnp.logical_not(inner))
        def _():
            def give(q):
                begin(q)
                j, r, c = place(q)
                outgoing[j, r] = stepped[j, r].astype(jnp.bfloat16)

                to_near(q).start()
                input_blocks(q)

            loop(0, steps, give)
            loop(0, steps, lambda q: to_near(q).wait_send())
            loop(0, steps, lambda q: back(q).wait_recv())

        @pl.when(inner)
        def _():
            def finish(q):
                j, r, c = place(q)
                to_far(q).wait_recv()
                emit(q, (j, r, c), stepped[j, r] + second_in[j, r].astype(jnp.float32))

            def merge(q):
                begin(q)
                j, r, c = place(q)
                to_near(q).wait_recv()
                own = stepped[j, r] + first_in[j, r].astype(jnp.float32)
                stepped[j, r] = own
                outgoing[j, r] = own.astype(jnp.bfloat16)
                to_far(q).start()

                @pl.when(q >= lag)
                def _():
                    finish(q - lag)

                input_blocks(q)

            loop(0, steps, merge)
            loop(steps - lag, steps, finish)

            def settle(q):
                j, r, c = place(q)
                to_far(q).wait_send()
                back(q).wait_send()
                pltpu.make_async_copy(total.at[j, r], total_hbm.at[j, r], out_sem.at[q]).wait()

            loop(0, steps, settle)
    else:
        def to_near(q, half):
            j, r, c = place(q, half)
            return remote(outgoing.at[j, r], first_in.at[j, r], send_a.at[q], recv_a.at[q], near)

        def to_far(q):
            j, r, c = place(q, low)
            return remote(outgoing.at[j, r], second_in.at[j, r], send_b.at[q], recv_b.at[q], far)

        def back(q, half):
            j, r, c = place(q, half)
            return remote(total.at[j, r], total_hbm.at[j, r], send_c.at[q], recv_c.at[q], near)

        def merge(q):
            j, r, c = place(q, low)
            to_near(q, low).wait_recv()
            both = stepped[j, r] + first_in[j, r].astype(jnp.float32)
            stepped[j, r] = both
            outgoing[j, r] = both.astype(jnp.bfloat16)
            to_far(q).start()

        def finish(q):
            j, r, c = place(q, low)
            to_far(q).wait_recv()
            emit(q, (j, r, c), stepped[j, r] + second_in[j, r].astype(jnp.float32))

        def give(j):
            take_grads(j)
            step_half(j, 1 - low)
            for i in range(parts):
                _, r, c = place(j * parts + i, 1 - low)
                outgoing[j, r] = stepped[j, r].astype(jnp.bfloat16)
                to_near(j * parts + i, 1 - low).start()
            if halves == 2:
                step_half(j, low)
            for i in range(parts):
                merge(j * parts + i)
            round_master(j)

        loop(0, n_cols, give)
        loop(0, n_blocks, input_block)
        loop(0, steps, finish)
        loop(0, steps, lambda q: to_far(q).wait_send())

        def settle(q):
            j, r, c = place(q, low)
            to_near(q, 1 - low).wait_send()
            back(q, low).wait_send()
            back(q, 1 - low).wait_recv()
            pltpu.make_async_copy(total.at[j, r], total_hbm.at[j, r], out_sem.at[q]).wait()

        loop(0, steps, settle)

    def settle_grads(j, carry):
        for d in range(1, n_tensor):
            grad_copy(j, d, True).wait_send()
        return carry

    lax.fori_loop(0, n_cols, settle_grads, 0)
    loop(0, n_blocks, lambda b: input_copy(b).wait())


def gossip(features, key_grad, shard, bit, top, n_tensor):
    tokens, width = features.shape
    columns = key_grad.shape[1]
    chain = bit == top - 1
    span = width if chain else width // 2
    parts, lag = (8, 3) if chain else (2, 0)
    if span // parts % 16:
        parts //= 2
    n_cols = columns // LANES
    steps = n_cols * parts
    dma = pltpu.SemaphoreType.DMA
    half, full = jnp.bfloat16, jnp.float32
    return pl.pallas_call(
        partial(kernel, bit, top, n_tensor, parts, lag),
        out_shape=(
            jax.ShapeDtypeStruct((n_cols, width, LANES), half),
            jax.ShapeDtypeStruct((tokens, width), half),
        ),
        in_specs=[pl.BlockSpec(memory_space=pl.ANY)] * 3,
        out_specs=[pl.BlockSpec(memory_space=pl.ANY)] * 2,
        scratch_shapes=[
            pltpu.VMEM((tokens, width), half),
            pltpu.VMEM((LANES, tokens), half),
            pltpu.VMEM((tokens, columns), half),
            pltpu.VMEM((width, columns), full),
            pltpu.VMEM((width, columns), half),
            pltpu.VMEM((n_cols, width, LANES), half),
            pltpu.VMEM((n_cols, width, LANES), half),
            pltpu.VMEM((n_cols, width, LANES), half),
            pltpu.VMEM((n_cols, width, LANES), full),
            pltpu.VMEM((n_cols, width, LANES), half),
            pltpu.VMEM((tokens, width), half),
            dma((LOADS + 2,)),
            dma((n_cols, n_tensor - 1)),
            dma((n_cols, n_tensor - 1)),
            dma((steps,)),
            dma((8,)),
            dma((steps,)), dma((steps,)), dma((steps,)), dma((steps,)), dma((steps,)), dma((steps,)),
        ],
        compiler_params=pltpu.CompilerParams(
            collective_id=bit, has_side_effects=True, vmem_limit_bytes=36 * 1024 * 1024
        ),
        name=f"gossip_{bit}",
    )(features, key_grad, shard)


def write_outputs(pieces, total_in, input_in, master_out, working_out, input_out, total, master, working, sem):
    n_cols, width, _ = total.shape
    rows = width // pieces
    tokens = input_in.shape[0]

    def copy(k, src, dst, i):
        return pltpu.make_async_copy(src, dst, sem.at[k, i])

    loads, stores = [], []
    for i in range(pieces):
        r = pl.ds(i * rows, rows)
        loads.append(copy(0, total_in.at[:, r], total.at[:, r], i))
        loads[i].start()
    for i in range(pieces):
        r = pl.ds(i * (tokens // pieces), tokens // pieces)
        stores.append(copy(1, input_in.at[r], input_out.at[r], i))
        stores[-1].start()
    for i in range(pieces):
        r = pl.ds(i * rows, rows)
        loads[i].wait()
        for j in range(n_cols):
            mean = 0.25 * total[j, i * rows:(i + 1) * rows, :].astype(jnp.float32)
            master[i * rows:(i + 1) * rows, j * LANES:(j + 1) * LANES] = mean
            working[i * rows:(i + 1) * rows, j * LANES:(j + 1) * LANES] = mean.astype(jnp.bfloat16)
        for k, src, dst in ((2, master, master_out), (3, working, working_out)):
            stores.append(copy(k, src.at[r], dst.at[r], i))
            stores[-1].start()
    for store in stores:
        store.wait()


def outputs(total, input_rows, pieces=5):
    n_cols, width, _ = total.shape
    columns = n_cols * LANES
    half, full = jnp.bfloat16, jnp.float32
    return pl.pallas_call(
        partial(write_outputs, pieces),
        out_shape=(
            jax.ShapeDtypeStruct((width, columns), full),
            jax.ShapeDtypeStruct((width, columns), half),
            jax.ShapeDtypeStruct(input_rows.shape, half),
        ),
        in_specs=[pl.BlockSpec(memory_space=pl.ANY)] * 2,
        out_specs=[pl.BlockSpec(memory_space=pl.ANY)] * 3,
        scratch_shapes=[
            pltpu.VMEM(total.shape, half),
            pltpu.VMEM((width, columns), full),
            pltpu.VMEM((width, columns), half),
            pltpu.SemaphoreType.DMA((4, pieces)),
        ],
        compiler_params=pltpu.CompilerParams(vmem_limit_bytes=24 * 1024 * 1024),
        name="write_outputs",
    )(total, input_rows)


def solution(mesh):
    n_tensor = mesh.shape["tensor"]
    top = mesh.shape["replica"].bit_length() - 2

    def local(features, key_grad, master, exponents):
        which = jnp.min(exponents)
        branches = [partial(gossip, bit=bit, top=top, n_tensor=n_tensor) for bit in range(top)]
        total, input_rows = lax.switch(which, branches, features, key_grad, master[0])
        new_master, new_working, input_grad = outputs(total, input_rows)
        return new_master[None], new_working[None], input_grad

    in_specs = (
        P("replica", "tensor"),
        P(("replica", "tensor"), None),
        P("replica", "tensor", None),
        P(),
    )
    out_specs = (P("replica", "tensor", None), P("replica", "tensor", None), P("replica", "tensor"))
    return jax.shard_map(local, mesh=mesh, in_specs=in_specs, out_specs=out_specs, check_vma=False)
```

```python
from functools import partial

import jax
import jax.numpy as jnp
from jax import lax
from jax.experimental import pallas as pl
from jax.experimental.pallas import tpu as pltpu
from jax.sharding import PartitionSpec as P

MESH = pl.DeviceIdType.MESH
step_rate = 0.2
LANES = 128
LOADS = 5


def remote(src, dst, send_sem, recv_sem, device):
    return pltpu.make_async_remote_copy(
        src_ref=src, dst_ref=dst, send_sem=send_sem, recv_sem=recv_sem,
        device_id=device, device_id_type=MESH,
    )


def kernel(
    bit, top, n_tensor, parts, lag,
    feat_hbm, grad_hbm, master_hbm,
    total_hbm, input_hbm,
    feat, grads_t, grads, master, working, outgoing, first_in, second_in, stepped, total, rows_out,
    load_sem, grad_send, grad_recv, out_sem, rows_sem,
    send_a, recv_a, send_b, recv_b, send_c, recv_c,
):
    replica, tensor = lax.axis_index("replica"), lax.axis_index("tensor")
    tokens, width = feat.shape
    columns = grads.shape[1]
    shard_tokens = grad_hbm.shape[0]
    n_cols = columns // LANES
    chain = bit == top - 1
    low = replica // (1 << bit) % 2
    high = replica // (1 << top) % 2
    near = {"replica": replica + (1 - 2 * low) * (1 << bit), "tensor": tensor}
    far_step = (1 - 2 * high) * (1 << top)
    if chain:
        inner = low != high
        far = {"replica": replica + (1 - 2 * high) * (1 << bit), "tensor": tensor}
    else:
        far = {"replica": replica + far_step, "tensor": tensor}

    def peer(d):
        return lax.rem(tensor + d, n_tensor)

    feat_loads = []
    for b in range(LOADS):
        block = pl.ds(b * (tokens // LOADS), tokens // LOADS)
        feat_loads.append(pltpu.make_async_copy(feat_hbm.at[block], feat.at[block], load_sem.at[b]))
    master_load = pltpu.make_async_copy(master_hbm, master, load_sem.at[LOADS])
    own_rows = pl.ds(pl.multiple_of(tensor * shard_tokens, 16), shard_tokens)
    own_grads = pltpu.make_async_copy(grad_hbm, grads.at[own_rows], load_sem.at[LOADS + 1])
    for load in feat_loads:
        load.start()
    own_grads.start()
    master_load.start()

    barrier = pltpu.get_barrier_semaphore()
    for d in range(1, n_tensor):
        pl.semaphore_signal(barrier, inc=1, device_id={"replica": replica, "tensor": peer(d)}, device_id_type=MESH)
    pl.semaphore_signal(barrier, inc=1, device_id=near, device_id_type=MESH)
    if chain:
        @pl.when(inner)
        def _():
            pl.semaphore_signal(barrier, inc=1, device_id=far, device_id_type=MESH)
            pl.semaphore_wait(barrier, n_tensor + 1)

        @pl.when(jnp.logical_not(inner))
        def _():
            pl.semaphore_wait(barrier, n_tensor)
    else:
        pl.semaphore_signal(barrier, inc=1, device_id=far, device_id_type=MESH)
        pl.semaphore_wait(barrier, n_tensor + 1)

    def grad_copy(j, d, sending):
        source = tensor if sending else lax.rem(tensor + n_tensor - d, n_tensor)
        cols = pl.ds(pl.multiple_of(j * LANES, LANES), LANES)
        rows = pl.ds(pl.multiple_of(source * shard_tokens, 16), shard_tokens)
        return remote(
            grad_hbm.at[:, cols], grads.at[rows, cols], grad_send.at[j, d - 1], grad_recv.at[j, d - 1],
            {"replica": replica, "tensor": peer(d)},
        )

    def send_grads(j, carry):
        for d in range(1, n_tensor):
            grad_copy(j, d, True).start()
        return carry

    send_grads(0, 0)

    for load in feat_loads:
        load.wait()
    own_grads.wait()
    master_load.wait()

    span = width if chain else width // 2
    rows = span // parts
    steps = n_cols * parts

    def place(q, half=None):
        j = q // parts
        i = q - j * parts
        start = i * rows if half is None else half * span + i * rows
        return j, pl.ds(pl.multiple_of(start, 16), rows), pl.ds(pl.multiple_of(j * LANES, LANES), LANES)

    def take_grads(j):
        for d in range(1, n_tensor):
            grad_copy(j, d, False).wait_recv()

        @pl.when(j + 1 < n_cols)
        def _():
            send_grads(j + 1, 0)

        c = pl.ds(pl.multiple_of(j * LANES, LANES), LANES)
        grads_t[...] = grads[:, c].T

    halves = 2 if width % (2 * LANES) == 0 else 1

    def step_half(j, half):
        size = width // halves
        r = pl.ds(pl.multiple_of(half * size, LANES), size) if halves == 2 else slice(None)
        c = pl.ds(pl.multiple_of(j * LANES, LANES), LANES)
        turned = jnp.dot(grads_t[...], feat[:, r], preferred_element_type=jnp.float32)
        stepped[j, r] = master[r, c] - step_rate * turned.T

    def round_master(j):
        c = pl.ds(pl.multiple_of(j * LANES, LANES), LANES)
        working[:, c] = master[:, c].astype(jnp.bfloat16)

    def begin(q):
        j = q // parts

        @pl.when(lax.rem(q, parts) == 0)
        def _():
            take_grads(j)
            round_master(j)
            step_half(j, 0)

        if halves == 2:
            @pl.when(lax.rem(q, parts) == parts // 2)
            def _():
                step_half(j, 1)

    def emit(q, at, value):
        j, r, c = at
        total[j, r] = value.astype(jnp.bfloat16)
        pltpu.make_async_copy(total.at[j, r], total_hbm.at[j, r], out_sem.at[q]).start()
        remote(total.at[j, r], total_hbm.at[j, r], send_c.at[q], recv_c.at[q], near).start()

    n_blocks = 8
    block_tokens = tokens // n_blocks

    def input_copy(b):
        r = pl.ds(pl.multiple_of(b * block_tokens, 16), block_tokens)
        return pltpu.make_async_copy(rows_out.at[r], input_hbm.at[r], rows_sem.at[b])

    def input_block(b):
        r = pl.ds(pl.multiple_of(b * block_tokens, 16), block_tokens)
        rows_out[r, :] = lax.dot_general(
            grads[r, :], working[...], (((1,), (1,)), ((), ())), preferred_element_type=jnp.float32
        ).astype(jnp.bfloat16)
        input_copy(b).start()

    def input_blocks(q):
        @pl.when(q >= steps - parts)
        def _():
            input_block(q - (steps - parts))

    def loop(begin, end, body):
        def run(q, carry):
            body(q)
            return carry

        lax.fori_loop(begin, end, run, 0)

    if chain:
        def to_near(q):
            j, r, c = place(q)
            return remote(outgoing.at[j, r], first_in.at[j, r], send_a.at[q], recv_a.at[q], near)

        def to_far(q):
            j, r, c = place(q)
            return remote(outgoing.at[j, r], second_in.at[j, r], send_b.at[q], recv_b.at[q], far)

        def back(q):
            j, r, c = place(q)
            return remote(total.at[j, r], total_hbm.at[j, r], send_c.at[q], recv_c.at[q], near)

        @pl.when(jnp.logical_not(inner))
        def _():
            def give(q):
                begin(q)
                j, r, c = place(q)
                outgoing[j, r] = stepped[j, r].astype(jnp.bfloat16)

                to_near(q).start()

            loop(0, steps, give)
            loop(0, n_blocks, input_block)
            loop(0, steps, lambda q: to_near(q).wait_send())
            loop(0, steps, lambda q: back(q).wait_recv())

        @pl.when(inner)
        def _():
            def finish(q):
                j, r, c = place(q)
                to_far(q).wait_recv()
                emit(q, (j, r, c), stepped[j, r] + second_in[j, r].astype(jnp.float32))

            def merge(q):
                begin(q)
                j, r, c = place(q)
                to_near(q).wait_recv()
                own = stepped[j, r] + first_in[j, r].astype(jnp.float32)
                stepped[j, r] = own
                outgoing[j, r] = own.astype(jnp.bfloat16)
                to_far(q).start()

                @pl.when(q >= lag)
                def _():
                    finish(q - lag)

                input_blocks(q)

            loop(0, steps, merge)
            loop(steps - lag, steps, finish)
            loop(parts, n_blocks, input_block)

            def settle(q):
                j, r, c = place(q)
                to_far(q).wait_send()
                back(q).wait_send()
                pltpu.make_async_copy(total.at[j, r], total_hbm.at[j, r], out_sem.at[q]).wait()

            loop(0, steps, settle)
    else:
        def to_near(q, half):
            j, r, c = place(q, half)
            return remote(outgoing.at[j, r], first_in.at[j, r], send_a.at[q], recv_a.at[q], near)

        def to_far(q):
            j, r, c = place(q, low)
            return remote(outgoing.at[j, r], second_in.at[j, r], send_b.at[q], recv_b.at[q], far)

        def back(q, half):
            j, r, c = place(q, half)
            return remote(total.at[j, r], total_hbm.at[j, r], send_c.at[q], recv_c.at[q], near)

        def merge(q):
            j, r, c = place(q, low)
            to_near(q, low).wait_recv()
            both = stepped[j, r] + first_in[j, r].astype(jnp.float32)
            stepped[j, r] = both
            outgoing[j, r] = both.astype(jnp.bfloat16)
            to_far(q).start()

        def finish(q):
            j, r, c = place(q, low)
            to_far(q).wait_recv()
            emit(q, (j, r, c), stepped[j, r] + second_in[j, r].astype(jnp.float32))

        def give(j):
            take_grads(j)
            step_half(j, 1 - low)
            for i in range(parts):
                _, r, c = place(j * parts + i, 1 - low)
                outgoing[j, r] = stepped[j, r].astype(jnp.bfloat16)
                to_near(j * parts + i, 1 - low).start()
            if halves == 2:
                step_half(j, low)
            for i in range(parts):
                merge(j * parts + i)
            round_master(j)

        loop(0, n_cols, give)
        loop(0, n_blocks, input_block)
        loop(0, steps, finish)
        loop(0, steps, lambda q: to_far(q).wait_send())

        def settle(q):
            j, r, c = place(q, low)
            to_near(q, 1 - low).wait_send()
            back(q, low).wait_send()
            back(q, 1 - low).wait_recv()
            pltpu.make_async_copy(total.at[j, r], total_hbm.at[j, r], out_sem.at[q]).wait()

        loop(0, steps, settle)

    def settle_grads(j, carry):
        for d in range(1, n_tensor):
            grad_copy(j, d, True).wait_send()
        return carry

    lax.fori_loop(0, n_cols, settle_grads, 0)
    loop(0, n_blocks, lambda b: input_copy(b).wait())


def gossip(features, key_grad, shard, bit, top, n_tensor):
    tokens, width = features.shape
    columns = key_grad.shape[1]
    chain = bit == top - 1
    span = width if chain else width // 2
    parts, lag = (4, 2) if chain else (2, 0)
    if span // parts % 16:
        parts //= 2
    n_cols = columns // LANES
    steps = n_cols * parts
    dma = pltpu.SemaphoreType.DMA
    half, full = jnp.bfloat16, jnp.float32
    return pl.pallas_call(
        partial(kernel, bit, top, n_tensor, parts, lag),
        out_shape=(
            jax.ShapeDtypeStruct((n_cols, width, LANES), half),
            jax.ShapeDtypeStruct((tokens, width), half),
        ),
        in_specs=[pl.BlockSpec(memory_space=pl.ANY)] * 3,
        out_specs=[pl.BlockSpec(memory_space=pl.ANY)] * 2,
        scratch_shapes=[
            pltpu.VMEM((tokens, width), half),
            pltpu.VMEM((LANES, tokens), half),
            pltpu.VMEM((tokens, columns), half),
            pltpu.VMEM((width, columns), full),
            pltpu.VMEM((width, columns), half),
            pltpu.VMEM((n_cols, width, LANES), half),
            pltpu.VMEM((n_cols, width, LANES), half),
            pltpu.VMEM((n_cols, width, LANES), half),
            pltpu.VMEM((n_cols, width, LANES), full),
            pltpu.VMEM((n_cols, width, LANES), half),
            pltpu.VMEM((tokens, width), half),
            dma((LOADS + 2,)),
            dma((n_cols, n_tensor - 1)),
            dma((n_cols, n_tensor - 1)),
            dma((steps,)),
            dma((8,)),
            dma((steps,)), dma((steps,)), dma((steps,)), dma((steps,)), dma((steps,)), dma((steps,)),
        ],
        compiler_params=pltpu.CompilerParams(
            collective_id=bit, has_side_effects=True, vmem_limit_bytes=36 * 1024 * 1024
        ),
        name=f"gossip_{bit}",
    )(features, key_grad, shard)


def write_outputs(pieces, total_in, input_in, master_out, working_out, input_out, total, master, working, sem):
    n_cols, width, _ = total.shape
    rows = width // pieces
    tokens = input_in.shape[0]

    def copy(k, src, dst, i):
        return pltpu.make_async_copy(src, dst, sem.at[k, i])

    loads, stores = [], []
    for i in range(pieces):
        r = pl.ds(i * rows, rows)
        loads.append(copy(0, total_in.at[:, r], total.at[:, r], i))
        loads[i].start()
    for i in range(pieces):
        r = pl.ds(i * (tokens // pieces), tokens // pieces)
        stores.append(copy(1, input_in.at[r], input_out.at[r], i))
        stores[-1].start()
    for i in range(pieces):
        r = pl.ds(i * rows, rows)
        loads[i].wait()
        for j in range(n_cols):
            mean = 0.25 * total[j, i * rows:(i + 1) * rows, :].astype(jnp.float32)
            master[i * rows:(i + 1) * rows, j * LANES:(j + 1) * LANES] = mean
            working[i * rows:(i + 1) * rows, j * LANES:(j + 1) * LANES] = mean.astype(jnp.bfloat16)
        for k, src, dst in ((2, master, master_out), (3, working, working_out)):
            stores.append(copy(k, src.at[r], dst.at[r], i))
            stores[-1].start()
    for store in stores:
        store.wait()


def outputs(total, input_rows, pieces=5):
    n_cols, width, _ = total.shape
    columns = n_cols * LANES
    half, full = jnp.bfloat16, jnp.float32
    return pl.pallas_call(
        partial(write_outputs, pieces),
        out_shape=(
            jax.ShapeDtypeStruct((width, columns), full),
            jax.ShapeDtypeStruct((width, columns), half),
            jax.ShapeDtypeStruct(input_rows.shape, half),
        ),
        in_specs=[pl.BlockSpec(memory_space=pl.ANY)] * 2,
        out_specs=[pl.BlockSpec(memory_space=pl.ANY)] * 3,
        scratch_shapes=[
            pltpu.VMEM(total.shape, half),
            pltpu.VMEM((width, columns), full),
            pltpu.VMEM((width, columns), half),
            pltpu.SemaphoreType.DMA((4, pieces)),
        ],
        compiler_params=pltpu.CompilerParams(vmem_limit_bytes=24 * 1024 * 1024),
        name="write_outputs",
    )(total, input_rows)


def solution(mesh):
    n_tensor = mesh.shape["tensor"]
    top = mesh.shape["replica"].bit_length() - 2

    def local(features, key_grad, master, exponents):
        which = jnp.min(exponents)
        branches = [partial(gossip, bit=bit, top=top, n_tensor=n_tensor) for bit in range(top)]
        total, input_rows = lax.switch(which, branches, features, key_grad, master[0])
        new_master, new_working, input_grad = outputs(total, input_rows)
        return new_master[None], new_working[None], input_grad

    in_specs = (
        P("replica", "tensor"),
        P(("replica", "tensor"), None),
        P("replica", "tensor", None),
        P(),
    )
    out_specs = (P("replica", "tensor", None), P("replica", "tensor", None), P("replica", "tensor"))
    return jax.shard_map(local, mesh=mesh, in_specs=in_specs, out_specs=out_specs, check_vma=False)
```
